512 devices in a mesh: dp: 512 (over y, z, x, core).
Axes of the slice: x: 4, y: 4, z: 16, core: 2. Of those that a mesh axis runs over, the one named last changes fastest.
Arguments:
- image_embed: float32 [131072, 1152], P('dp'), may hold values from -0.1875 to 0.1875
- text_embed: float32 [131072, 1152], P('dp'), may hold values from -0.1875 to 0.1875
- logit_scale: float32 [1], replicated, may hold values from 4 to 16
- logit_bias: float32 [1], replicated, may hold values from -3 to -0.5
Outputs:
- grad_image: float32 [131072, 1152], P('dp')
- grad_text: float32 [131072, 1152], P('dp')
The draws below stay inside these ranges and needn't reach their ends.
All inputs are finite; a program needn't handle non-finite values.
Results may differ from the reference program's by a relative error of at most 0.0001.
Values sent between devices are 32-bit elements; how exact they have to be, the bound alone decides.
No kernel may reach another device: no remote copies, remote signals or barrier semaphores. Data moves between devices by JAX's collectives and lax.ppermute only.
A program may use at most 64 MiB of HBM per device.

```python
import math
import jax
import jax.numpy as jnp
from jax import lax

D = 1152
ROWS = 256
REACH = 2
PAIRS = 131072
N_DP = 512


def shard_levels(stream_key, dims, split, low, top_value):
    gain, own = 1.0, jax.random.fold_in(stream_key, 6)
    for axis_at, shards_of in split:
        heights = jnp.exp(jax.random.uniform(jax.random.fold_in(own, axis_at), (shards_of,), jnp.float32, low / len(split), top_value / len(split)))
        gain = gain * jnp.repeat(heights, dims[axis_at] // shards_of).reshape([-1 if axis == axis_at else 1 for axis in range(len(dims))])
    return gain


def centred(rng, dims, scale, bound, split=(), dtype=jnp.bfloat16):
    drawn = jax.random.normal(rng, dims, jnp.float32) * scale
    if len(split) > 0:
        drawn = shard_levels(rng, dims, split, -0.22, 0.18) * drawn
    return jnp.clip(drawn, min=-bound, max=bound).astype(dtype)


def setup_inputs(seed: int = 0) -> dict:
    streams_of = jax.random.split(jax.random.key(seed), 5)
    return {
        "image_embed": centred(streams_of[0], (PAIRS, D), D ** -0.5, 0.1875, ((0, 512),), jnp.float32),
        "text_embed": centred(streams_of[1], (PAIRS, D), D ** -0.5, 0.1875, ((0, 512),), jnp.float32),
        "logit_scale": jnp.clip(jnp.exp(jax.random.uniform(streams_of[2], (1,), jnp.float32, math.log(4.0), math.log(16.0))), 4.0, 16.0),
        "logit_bias": jnp.clip(jax.random.uniform(streams_of[3], (1,), jnp.float32, -3.0, -0.5), -3.0, -0.5),
    }


def normalize(raw):
    norm = jnp.sqrt(lax.optimization_barrier(jnp.sum(raw * raw, axis=1, keepdims=True)) + 1e-06)
    return (raw / norm, norm)

def project_back(hat, grad_hat, norm):
    inner = lax.optimization_barrier(jnp.sum(hat * grad_hat, axis=1, keepdims=True))
    return (grad_hat - hat * inner) / norm

def reference(image_embed, text_embed, logit_scale, logit_bias):
    img_hat, img_norm = normalize(image_embed)
    txt_hat, txt_norm = normalize(text_embed)
    scale = logit_scale[0]
    bias = logit_bias[0]
    img_blocks = img_hat.reshape(N_DP, ROWS, D)
    txt_blocks = txt_hat.reshape(N_DP, ROWS, D)
    ident = (lax.broadcasted_iota(jnp.int32, (ROWS, ROWS), 0) == lax.broadcasted_iota(jnp.int32, (ROWS, ROWS), 1)).astype(jnp.float32)
    img_grad = jnp.zeros((N_DP, ROWS, D), jnp.float32)
    txt_grad = jnp.zeros((N_DP, ROWS, D), jnp.float32)
    for offset in range(-REACH, REACH + 1):
        right = jnp.roll(txt_blocks, -offset, axis=0)
        logits = scale * jnp.einsum('pid,pjd->pij', img_blocks, right, precision=lax.Precision.HIGHEST) + bias
        if offset == 0:
            sign = 2.0 * ident - 1.0
        else:
            sign = -jnp.ones((ROWS, ROWS), jnp.float32)
        coeff = -sign * jax.nn.sigmoid(-sign * logits)
        img_grad = img_grad + scale * jnp.einsum('pij,pjd->pid', coeff, right, precision=lax.Precision.HIGHEST)
        partial_grad = scale * jnp.einsum('pij,pid->pjd', coeff, img_blocks, precision=lax.Precision.HIGHEST)
        txt_grad = txt_grad + jnp.roll(partial_grad, offset, axis=0)
    grad_image = project_back(img_hat, img_grad.reshape(PAIRS, D), img_norm)
    grad_text = project_back(txt_hat, txt_grad.reshape(PAIRS, D), txt_norm)
    return (grad_image, grad_text)
```

```python
import functools

import jax
import jax.numpy as jnp
from jax import lax
from jax.experimental import pallas as pl
from jax.experimental.pallas import tpu as pltpu
from jax.sharding import PartitionSpec as P

F32 = jnp.float32
BF16 = jnp.bfloat16
VMEM = pl.BlockSpec(memory_space=pltpu.VMEM)
SMEM = pl.BlockSpec(memory_space=pltpu.SMEM)
NT = (((1,), (1,)), ((), ()))
NN = (((1,), (0,)), ((), ()))


def split(value):
    hi = value.astype(BF16)
    return hi, (value - hi.astype(F32)).astype(BF16)


def product(left, right, dims):
    mul = functools.partial(
        lax.dot_general, dimension_numbers=dims, preferred_element_type=F32
    )
    (lh, ll), (rh, rl) = left, right
    return mul(lh, rh) + (mul(lh, rl) + mul(ll, rh))


def unit(raw):
    inv = 1.0 / jnp.sqrt(jnp.sum(raw * raw, axis=1, keepdims=True) + 1e-06)
    return raw * inv, inv


def tile_grad(x, y, scale, bias, matching=False):
    logits = scale * product(x, y, NT) + bias
    if matching:
        diag = lax.broadcasted_iota(jnp.int32, logits.shape, 0) == (
            lax.broadcasted_iota(jnp.int32, logits.shape, 1)
        )
        sign = jnp.where(diag, -1.0, 1.0)
        coeff = sign * jax.nn.sigmoid(sign * logits)
    else:
        coeff = jax.nn.sigmoid(logits)
    return product(split(coeff), y, NN)


def own_kernel(scale, bias, img, txt, ihat, that, ihat_a, ihat_b, stack, *outs):
    (iinv, ihi, ilo, igrad, tinv, thi, tlo, tgrad) = outs
    rows, first = img.shape[0], ihat_a.shape[0]
    stack[:rows], iinv[...] = unit(img[...])
    stack[rows:], tinv[...] = unit(txt[...])
    ihat_a[...] = stack[:first]
    ihat_b[...] = stack[first:rows]
    ihat[...] = stack[:rows]
    that[...] = stack[rows:]
    ihi[...], ilo[...] = split(stack[:rows])
    thi[...], tlo[...] = split(stack[rows:])
    x, y = (ihi[...], ilo[...]), (thi[...], tlo[...])
    igrad[...] = tile_grad(x, y, scale[0], bias[0], True)
    tgrad[...] = tile_grad(y, x, scale[0], bias[0], True)


def raw_kernel(scale, bias, hi, lo, raw, grad, hat, total):
    hat[...] = unit(raw[...])[0]
    total[...] = grad[...] + tile_grad(
        (hi[...], lo[...]), split(hat[...]), scale[0], bias[0]
    )


def tile_kernel(scale, bias, hi, lo, hat, grad, total):
    total[...] = grad[...] + tile_grad(
        (hi[...], lo[...]), split(hat[...]), scale[0], bias[0]
    )


def stack_kernel(scale, bias, hi, lo, img, txt, grad, stack, total):
    stack[: img.shape[0]] = img[...]
    stack[img.shape[0] :] = txt[...]
    tile_kernel(scale, bias, hi, lo, img, grad, total)


def pair_kernel(scale, bias, ihi, ilo, thi, tlo, stack, igrad, tgrad, itotal, ttotal):
    rows = igrad.shape[0]
    tile_kernel(scale, bias, ihi, ilo, stack.at[rows:], igrad, itotal)
    tile_kernel(scale, bias, thi, tlo, stack.at[:rows], tgrad, ttotal)


def project(out, total, hat, inv):
    inner = jnp.sum(hat * total, axis=1, keepdims=True)
    out[...] = (total - hat * inner) * inv


def cross_kernel(
    scale, bias, ihi, ilo, thi, tlo, stack, igrad, tgrad, own, iinv, out, ttotal
):
    rows = igrad.shape[0]
    y = split(stack[rows:])
    total = igrad[...] + tile_grad((ihi[...], ilo[...]), y, scale[0], bias[0])
    project(out, scale[0] * total, own[:rows], iinv[...])
    tile_kernel(scale, bias, thi, tlo, stack.at[:rows], tgrad, ttotal)


def last_kernel(scale, bias, hi, lo, hat, grad, own, inv, out):
    y = split(hat[...])
    total = grad[...] + tile_grad((hi[...], lo[...]), y, scale[0], bias[0])
    project(out, scale[0] * total, own[...], inv[...])


def call(kernel, name, operands, outs, flops=1):
    return pl.pallas_call(
        kernel,
        name=name,
        out_shape=outs,
        in_specs=[SMEM, SMEM] + [VMEM] * (len(operands) - 2),
        out_specs=jax.tree.map(lambda _: VMEM, outs),
        compiler_params=pltpu.CompilerParams(vmem_limit_bytes=24 * 2**20),
        cost_estimate=pl.CostEstimate(flops=flops, bytes_accessed=0, transcendentals=0),
    )(*operands)


def body(image_embed, text_embed, logit_scale, logit_bias):
    rows, width = image_embed.shape
    first = rows // 2
    size = lax.axis_size("dp")

    def shape(height, wide=width, kind=F32):
        return jax.ShapeDtypeStruct((height, wide), kind)

    one, both = shape(rows), shape(2 * rows)
    state = (shape(rows, 1), shape(rows, kind=BF16), shape(rows, kind=BF16), one)
    tb = (logit_scale, logit_bias)

    def outward(block):
        return lax.ppermute(
            block, "dp", [(d, (d + (2 if d % 2 else -2)) % size) for d in range(size)]
        )

    def inward(block):
        return lax.ppermute(
            block, "dp", [(d, (d + (-2 if d % 2 else 2)) % size) for d in range(size)]
        )

    def swap(block):
        return lax.ppermute(block, "dp", [(d, d ^ 1) for d in range(size)])

    def after(*values):
        return lax.optimization_barrier(values)

    near_txt = outward(text_embed)
    ihat, that, ihat_a, ihat_b, own, *rest = call(
        own_kernel,
        "own_tiles",
        (*tb, image_embed, text_embed),
        (one, one, shape(first), shape(rows - first), both, *state, *state),
    )
    iinv, ihi, ilo, igrad, tinv, thi, tlo, tgrad = rest
    img, txt = (ihi, ilo), (thi, tlo)
    pair = swap(own)
    near_img = outward(ihat)
    far_txt = inward(that)

    near_txt, igrad = call(
        raw_kernel, "near_text", (*tb, *img, near_txt, igrad), (one, one), 10**11
    )
    ihat_a, igrad = after(ihat_a, igrad)
    far_img_a = inward(ihat_a)
    igrad, tgrad = call(
        pair_kernel, "pair_tiles", (*tb, *img, *txt, pair, igrad, tgrad), (one, one)
    )
    cross, tgrad = call(
        stack_kernel, "near_image", (*tb, *txt, near_img, near_txt, tgrad), (both, one)
    )
    ihat_b, tgrad = after(ihat_b, tgrad)
    cross = swap(cross)
    far_img_b = inward(ihat_b)
    igrad, tgrad = after(igrad, tgrad)
    igrad = call(tile_kernel, "far_text", (*tb, *img, far_txt, igrad), one)
    igrad, tgrad = after(igrad, tgrad)
    tgrad = call(tile_kernel, "far_image", (*tb, *txt, far_img_a, tgrad), one, 10**11)
    grad_image, tgrad = call(
        cross_kernel,
        "cross_tiles",
        (*tb, *img, *txt, cross, igrad, tgrad, own, iinv),
        (one, one),
    )
    grad_text = call(
        last_kernel, "last_image", (*tb, *txt, far_img_b, tgrad, that, tinv), one
    )
    return grad_image, grad_text


def solution(mesh):
    return jax.shard_map(
        body,
        mesh=mesh,
        in_specs=(P("dp", None), P("dp", None), P(), P()),
        out_specs=(P("dp", None), P("dp", None)),
        check_vma=False,
    )
```

```python
import functools

import jax
import jax.numpy as jnp
from jax import lax
from jax.experimental import pallas as pl
from jax.experimental.pallas import tpu as pltpu
from jax.sharding import PartitionSpec as P

F32 = jnp.float32
BF16 = jnp.bfloat16
VMEM = pl.BlockSpec(memory_space=pltpu.VMEM)
SMEM = pl.BlockSpec(memory_space=pltpu.SMEM)
HBM = pl.BlockSpec(memory_space=pltpu.HBM)
PARTS = 4
COLUMNS = 256
NT = (((1,), (1,)), ((), ()))
NN = (((1,), (0,)), ((), ()))


def split(value):
    hi = value.astype(BF16)
    return hi, (value - hi.astype(F32)).astype(BF16)


def product(left, right, dims):
    mul = functools.partial(
        lax.dot_general, dimension_numbers=dims, preferred_element_type=F32
    )
    (lh, ll), (rh, rl) = left, right
    return mul(lh, rh) + (mul(lh, rl) + mul(ll, rh))


def unit(raw):
    inv = 1.0 / jnp.sqrt(jnp.sum(raw * raw, axis=1, keepdims=True) + 1e-06)
    return raw * inv, inv


def tile_grad(x, y, scale, bias, matching=False):
    logits = scale * product(x, y, NT) + bias
    if matching:
        diag = lax.broadcasted_iota(jnp.int32, logits.shape, 0) == (
            lax.broadcasted_iota(jnp.int32, logits.shape, 1)
        )
        sign = jnp.where(diag, -1.0, 1.0)
        coeff = sign * jax.nn.sigmoid(sign * logits)
    else:
        coeff = jax.nn.sigmoid(logits)
    return product(split(coeff), y, NN)


def unit_kernel(img_in, txt_in, ihat, that, both, *refs):
    (iinv, ihi, ilo, tinv, thi, tlo, raw, sems) = refs
    rows = ihat.shape[0]
    part = rows // PARTS
    copies = []
    for n, source in enumerate((img_in, txt_in)):
        for k in range(PARTS):
            copies.append(
                pltpu.make_async_copy(
                    source.at[pl.ds(k * part, part)],
                    raw.at[pl.ds(n * rows + k * part, part)],
                    sems.at[n, k],
                )
            )
    for copy in copies:
        copy.start()
    for n, (hat, inv, hi, lo) in enumerate(((ihat, iinv, ihi, ilo), (that, tinv, thi, tlo))):
        for copy in copies[n * PARTS : (n + 1) * PARTS]:
            copy.wait()
        hat[...], inv[...] = unit(raw[n * rows : (n + 1) * rows])
        both[n * rows : (n + 1) * rows] = hat[...]
        hi[...], lo[...] = split(hat[...])


def own_kernel(scale, bias, ihi, ilo, thi, tlo, igrad, tgrad):
    x, y = (ihi[...], ilo[...]), (thi[...], tlo[...])
    igrad[...] = tile_grad(x, y, scale[0], bias[0], True)
    tgrad[...] = tile_grad(y, x, scale[0], bias[0], True)


def tile_kernel(scale, bias, hi, lo, hat, grad, total):
    total[...] = grad[...] + tile_grad(
        (hi[...], lo[...]), split(hat[...]), scale[0], bias[0]
    )


def raw_kernel(scale, bias, hi, lo, raw, grad, hat, total):
    hat[...] = unit(raw[...])[0]
    tile_kernel(scale, bias, hi, lo, hat, grad, total)


def pair_kernel(scale, bias, ihi, ilo, thi, tlo, both, igrad, tgrad, itotal, ttotal):
    rows = igrad.shape[0]
    tile_kernel(scale, bias, ihi, ilo, both.at[rows:], igrad, itotal)
    tile_kernel(scale, bias, thi, tlo, both.at[:rows], tgrad, ttotal)


def cross_kernel(scale, bias, hi, lo, hat, grad, own, total, inner):
    tile_kernel(scale, bias, hi, lo, hat, grad, total)
    inner[...] = jnp.sum(own[...] * total[...], axis=1, keepdims=True)


def last_kernel(scale, bias, hi, lo, hat, grad, own, inner, inv, out, part, sems):
    y = split(hat[...])
    dots = product((hi[...], lo[...]), y, NT)
    coeff = jax.nn.sigmoid(scale[0] * dots + bias[0])
    along = inner[...] + jnp.sum(coeff * dots, axis=1, keepdims=True)
    factor = scale[0] * inv[...]
    coeff = split(coeff)
    copies = []
    width = hat.shape[1]
    for at in range(0, width, COLUMNS):
        here = slice(at, min(at + COLUMNS, width))
        total = grad[:, here] + product(coeff, [half[:, here] for half in y], NN)
        part[:, here] = (total - own[:, here] * along) * factor
        wide = pl.ds(at, here.stop - at)
        copies.append(
            pltpu.make_async_copy(
                part.at[:, wide], out.at[:, wide], sems.at[at // COLUMNS]
            )
        )
        copies[-1].start()
    for copy in copies:
        copy.wait()


def call(kernel, name, operands, outs, scalars=2, spec=VMEM, out_spec=VMEM, **extra):
    return pl.pallas_call(
        kernel,
        name=name,
        out_shape=outs,
        in_specs=[SMEM] * scalars + [spec] * (len(operands) - scalars),
        out_specs=jax.tree.map(lambda _: out_spec, outs),
        compiler_params=pltpu.CompilerParams(vmem_limit_bytes=24 * 2**20),
        cost_estimate=pl.CostEstimate(flops=2 * 10**10, bytes_accessed=0, transcendentals=0),
        **extra,
    )(*operands)


def body(image_embed, text_embed, logit_scale, logit_bias):
    rows, width = image_embed.shape
    size = lax.axis_size("dp")

    def shape(height, wide=width, kind=F32):
        return jax.ShapeDtypeStruct((height, wide), kind)

    one = shape(rows)
    column = shape(rows, 1)
    state = (column, shape(rows, kind=BF16), shape(rows, kind=BF16))
    tb = (logit_scale, logit_bias)

    def outward(block):
        return lax.ppermute(
            block, "dp", [(d, (d + (2 if d % 2 else -2)) % size) for d in range(size)]
        )

    def inward(block):
        return lax.ppermute(
            block, "dp", [(d, (d + (-2 if d % 2 else 2)) % size) for d in range(size)]
        )

    def swap(block):
        return lax.ppermute(block, "dp", [(d, d ^ 1) for d in range(size)])

    def last(name, *operands):
        return call(
            last_kernel,
            name,
            (*tb, *operands),
            one,
            out_spec=HBM,
            scratch_shapes=[
                pltpu.VMEM((rows, width), F32),
                pltpu.SemaphoreType.DMA((pl.cdiv(width, COLUMNS),)),
            ],
        )

    def after(*values):
        return lax.optimization_barrier(values)

    near_txt = outward(text_embed)
    in_hbm = [
        pltpu.with_memory_space_constraint(raw, pltpu.HBM)
        for raw in (image_embed, text_embed)
    ]
    ihat, that, both, *rest = call(
        unit_kernel,
        "unit_rows",
        in_hbm,
        (one, one, shape(2 * rows), *state, *state),
        scalars=0,
        spec=HBM,
        scratch_shapes=[
            pltpu.VMEM((2 * rows, width), F32),
            pltpu.SemaphoreType.DMA((2, PARTS)),
        ],
    )
    iinv, ihi, ilo, tinv, thi, tlo = rest
    img, txt = (ihi, ilo), (thi, tlo)
    near_img = outward(ihat)
    pair = swap(both)
    igrad, tgrad = call(own_kernel, "own_tiles", (*tb, *img, *txt), (one, one))

    that_late, igrad, tgrad = after(that, igrad, tgrad)
    far_txt = inward(that_late)
    near_txt, igrad = call(
        raw_kernel, "near_text", (*tb, *img, near_txt, igrad), (one, one)
    )
    ihat_late, near_txt, igrad = after(ihat, near_txt, igrad)
    far_img = inward(ihat_late)
    cross_txt = swap(near_txt)
    igrad, tgrad = call(
        pair_kernel, "pair_tiles", (*tb, *img, *txt, pair, igrad, tgrad), (one, one)
    )
    igrad, inner_img = call(
        cross_kernel, "cross_text", (*tb, *img, cross_txt, igrad, ihat), (one, column)
    )

    near_img, igrad = after(near_img, igrad)
    cross_img = swap(near_img)
    tgrad = call(tile_kernel, "near_image", (*tb, *txt, near_img, tgrad), one)

    far_txt, igrad, tgrad = after(far_txt, igrad, tgrad)
    grad_image = last("last_text", *img, far_txt, igrad, ihat, inner_img, iinv)
    cross_img, grad_image = after(cross_img, grad_image)
    tgrad, inner_txt = call(
        cross_kernel, "cross_image", (*tb, *txt, cross_img, tgrad, that), (one, column)
    )
    grad_text = last("last_image", *txt, far_img, tgrad, that, inner_txt, tinv)
    return grad_image, grad_text


def solution(mesh):
    return jax.shard_map(
        body,
        mesh=mesh,
        in_specs=(P("dp", None), P("dp", None), P(), P()),
        out_specs=(P("dp", None), P("dp", None)),
        check_vma=False,
    )
```

```python
import functools

import jax
import jax.numpy as jnp
from jax import lax
from jax.experimental import pallas as pl
from jax.experimental.pallas import tpu as pltpu
from jax.sharding import PartitionSpec as P

F32 = jnp.float32
BF16 = jnp.bfloat16
VMEM = pl.BlockSpec(memory_space=pltpu.VMEM)
SMEM = pl.BlockSpec(memory_space=pltpu.SMEM)
HBM = pl.BlockSpec(memory_space=pltpu.HBM)
PARTS = 4
COLUMNS = 256
NT = (((1,), (1,)), ((), ()))
NN = (((1,), (0,)), ((), ()))


def split(value):
    hi = value.astype(BF16)
    return hi, (value - hi.astype(F32)).astype(BF16)


def product(left, right, dims):
    mul = functools.partial(
        lax.dot_general, dimension_numbers=dims, preferred_element_type=F32
    )
    (lh, ll), (rh, rl) = left, right
    return mul(lh, rh) + (mul(lh, rl) + mul(ll, rh))


def unit(raw):
    inv = 1.0 / jnp.sqrt(jnp.sum(raw * raw, axis=1, keepdims=True) + 1e-06)
    return raw * inv, inv


def tile_grad(x, y, scale, bias, matching=False):
    logits = scale * product(x, y, NT) + bias
    if matching:
        diag = lax.broadcasted_iota(jnp.int32, logits.shape, 0) == (
            lax.broadcasted_iota(jnp.int32, logits.shape, 1)
        )
        sign = jnp.where(diag, -1.0, 1.0)
        coeff = sign * jax.nn.sigmoid(sign * logits)
    else:
        coeff = jax.nn.sigmoid(logits)
    return product(split(coeff), y, NN)


def unit_kernel(img_in, txt_in, ihat, that, both, ihat_a, ihat_b, *refs):
    (iinv, ihi, ilo, tinv, thi, tlo, raw, sems) = refs
    rows = ihat.shape[0]
    part = rows // PARTS
    copies = []
    for n, source in enumerate((img_in, txt_in)):
        for k in range(PARTS):
            copies.append(
                pltpu.make_async_copy(
                    source.at[pl.ds(k * part, part)],
                    raw.at[pl.ds(n * rows + k * part, part)],
                    sems.at[n, k],
                )
            )
    for copy in copies:
        copy.start()
    for n, (hat, inv, hi, lo) in enumerate(((ihat, iinv, ihi, ilo), (that, tinv, thi, tlo))):
        for copy in copies[n * PARTS : (n + 1) * PARTS]:
            copy.wait()
        hat[...], inv[...] = unit(raw[n * rows : (n + 1) * rows])
        both[n * rows : (n + 1) * rows] = hat[...]
        hi[...], lo[...] = split(hat[...])
        if n == 0:
            ihat_a[...] = hat[: ihat_a.shape[0]]
            ihat_b[...] = hat[ihat_a.shape[0] :]


def own_kernel(scale, bias, ihi, ilo, thi, tlo, igrad, tgrad):
    x, y = (ihi[...], ilo[...]), (thi[...], tlo[...])
    igrad[...] = tile_grad(x, y, scale[0], bias[0], True)
    tgrad[...] = tile_grad(y, x, scale[0], bias[0], True)


def tile_kernel(scale, bias, hi, lo, hat, grad, total):
    total[...] = grad[...] + tile_grad(
        (hi[...], lo[...]), split(hat[...]), scale[0], bias[0]
    )


def near_kernel(raw, hat):
    hat[...] = unit(raw[...])[0]


def pair_kernel(scale, bias, ihi, ilo, thi, tlo, both, igrad, tgrad, own, *outs):
    itotal, ttotal, inner = outs
    rows = igrad.shape[0]
    cross_kernel(scale, bias, ihi, ilo, both.at[rows:], igrad, own, itotal, inner)
    tile_kernel(scale, bias, thi, tlo, both.at[:rows], tgrad, ttotal)


def cross_kernel(scale, bias, hi, lo, hat, grad, own, total, inner):
    tile_kernel(scale, bias, hi, lo, hat, grad, total)
    inner[...] = jnp.sum(own[...] * total[...], axis=1, keepdims=True)


def stacked(hi, lo, y_hi, y_lo, scale, bias):
    rows = y_hi.shape[0]
    mul = functools.partial(lax.dot_general, preferred_element_type=F32)
    both = mul(hi, jnp.concatenate([y_hi, y_lo], axis=0), NT)
    dots = both[:, :rows] + (both[:, rows:] + mul(lo, y_hi, NT))
    coeff = jax.nn.sigmoid(scale * dots + bias)
    top = coeff.astype(BF16).astype(F32)
    left = jnp.concatenate([top, top, coeff - top], axis=1).astype(BF16)
    right = jnp.concatenate([y_hi, y_lo, y_hi], axis=0)
    return dots, coeff, lambda here: mul(left, right[:, here], NN)


def last_kernel(scale, bias, hi, lo, hat, grad, own, inner, inv, out, part, sems):
    y = split(hat[...])
    if 3 * hat.shape[0] <= hi.shape[0]:
        dots, coeff, columns = stacked(hi[...], lo[...], *y, scale[0], bias[0])
    else:
        dots = product((hi[...], lo[...]), y, NT)
        coeff = jax.nn.sigmoid(scale[0] * dots + bias[0])
        halves = split(coeff)
        columns = lambda here: product(halves, [half[:, here] for half in y], NN)
    along = inner[...] + jnp.sum(coeff * dots, axis=1, keepdims=True)
    factor = scale[0] * inv[...]
    copies = []
    width = hat.shape[1]
    for at in range(0, width, COLUMNS):
        here = slice(at, min(at + COLUMNS, width))
        total = grad[:, here] + columns(here)
        part[:, here] = (total - own[:, here] * along) * factor
        wide = pl.ds(at, here.stop - at)
        copies.append(
            pltpu.make_async_copy(
                part.at[:, wide], out.at[:, wide], sems.at[at // COLUMNS]
            )
        )
        copies[-1].start()
    for copy in copies:
        copy.wait()


def call(kernel, name, operands, outs, scalars=2, spec=VMEM, out_spec=VMEM, **extra):
    return pl.pallas_call(
        kernel,
        name=name,
        out_shape=outs,
        in_specs=[SMEM] * scalars + [spec] * (len(operands) - scalars),
        out_specs=jax.tree.map(lambda _: out_spec, outs),
        compiler_params=pltpu.CompilerParams(vmem_limit_bytes=24 * 2**20),
        cost_estimate=pl.CostEstimate(flops=2 * 10**10, bytes_accessed=0, transcendentals=0),
        **extra,
    )(*operands)


def body(image_embed, text_embed, logit_scale, logit_bias):
    rows, width = image_embed.shape
    size = lax.axis_size("dp")

    def shape(height, wide=width, kind=F32):
        return jax.ShapeDtypeStruct((height, wide), kind)

    one = shape(rows)
    tail = rows // 4
    column = shape(rows, 1)
    state = (column, shape(rows, kind=BF16), shape(rows, kind=BF16))
    tb = (logit_scale, logit_bias)

    def outward(block):
        return lax.ppermute(
            block, "dp", [(d, (d + (2 if d % 2 else -2)) % size) for d in range(size)]
        )

    def inward(block):
        return lax.ppermute(
            block, "dp", [(d, (d + (-2 if d % 2 else 2)) % size) for d in range(size)]
        )

    def swap(block):
        return lax.ppermute(block, "dp", [(d, d ^ 1) for d in range(size)])

    def last(name, *operands):
        return call(
            last_kernel,
            name,
            (*tb, *operands),
            one,
            out_spec=HBM,
            scratch_shapes=[
                pltpu.VMEM((rows, width), F32),
                pltpu.SemaphoreType.DMA((pl.cdiv(width, COLUMNS),)),
            ],
        )

    def after(*values):
        return lax.optimization_barrier(values)

    near_txt = outward(text_embed)
    in_hbm = [
        pltpu.with_memory_space_constraint(raw, pltpu.HBM)
        for raw in (image_embed, text_embed)
    ]
    ihat, that, both, ihat_a, ihat_b, *rest = call(
        unit_kernel,
        "unit_rows",
        in_hbm,
        (one, one, shape(2 * rows), shape(rows - tail), shape(tail), *state, *state),
        scalars=0,
        spec=HBM,
        scratch_shapes=[
            pltpu.VMEM((2 * rows, width), F32),
            pltpu.SemaphoreType.DMA((2, PARTS)),
        ],
    )
    iinv, ihi, ilo, tinv, thi, tlo = rest
    img, txt = (ihi, ilo), (thi, tlo)
    near_img = outward(ihat)
    igrad, tgrad = call(own_kernel, "own_tiles", (*tb, *img, *txt), (one, one))

    that_late, igrad, tgrad = after(that, igrad, tgrad)
    far_txt = inward(that_late)
    near_txt, igrad = after(near_txt, igrad)
    near_txt = call(near_kernel, "near_rows", (near_txt,), one, scalars=0)
    both, near_txt = after(both, near_txt)
    cross_txt = swap(near_txt)
    pair = swap(both)
    igrad = call(tile_kernel, "near_text", (*tb, *img, near_txt, igrad), one)
    igrad = call(tile_kernel, "cross_text", (*tb, *img, cross_txt, igrad), one)
    ihat_a, ihat_b, igrad = after(ihat_a, ihat_b, igrad)
    far_img_a = inward(ihat_a)
    far_img_b = inward(ihat_b)
    igrad, tgrad, inner_img = call(
        pair_kernel,
        "pair_tiles",
        (*tb, *img, *txt, pair, igrad, tgrad, ihat),
        (one, one, column),
    )

    near_img, igrad = after(near_img, igrad)
    cross_img = swap(near_img)
    tgrad = call(tile_kernel, "near_image", (*tb, *txt, near_img, tgrad), one)

    far_txt, igrad, tgrad = after(far_txt, igrad, tgrad)
    grad_image = last("last_text", *img, far_txt, igrad, ihat, inner_img, iinv)
    cross_img, grad_image = after(cross_img, grad_image)
    tgrad = call(tile_kernel, "cross_image", (*tb, *txt, cross_img, tgrad), one)
    tgrad, inner_txt = call(
        cross_kernel, "far_image", (*tb, *txt, far_img_a, tgrad, that), (one, column)
    )
    grad_text = last("last_image", *txt, far_img_b, tgrad, that, inner_txt, tinv)
    return grad_image, grad_text


def solution(mesh):
    return jax.shard_map(
        body,
        mesh=mesh,
        in_specs=(P("dp", None), P("dp", None), P(), P()),
        out_specs=(P("dp", None), P("dp", None)),
        check_vma=False,
    )
```

```python
import functools

import jax
import jax.numpy as jnp
from jax import lax
from jax.experimental import pallas as pl
from jax.experimental.pallas import tpu as pltpu
from jax.sharding import PartitionSpec as P

F32 = jnp.float32
BF16 = jnp.bfloat16
VMEM = pl.BlockSpec(memory_space=pltpu.VMEM)
SMEM = pl.BlockSpec(memory_space=pltpu.SMEM)
HBM = pl.BlockSpec(memory_space=pltpu.HBM)
PARTS = 4
COLUMNS = 256
SEAM = 128
LATE = ("last_text", "cross_image", "far_image")
NT = (((1,), (1,)), ((), ()))
NN = (((1,), (0,)), ((), ()))


def split(value):
    hi = value.astype(BF16)
    return hi, (value - hi.astype(F32)).astype(BF16)


def product(left, right, dims):
    mul = functools.partial(
        lax.dot_general, dimension_numbers=dims, preferred_element_type=F32
    )
    (lh, ll), (rh, rl) = left, right
    return mul(lh, rh) + (mul(lh, rl) + mul(ll, rh))


def unit(raw):
    inv = 1.0 / jnp.sqrt(jnp.sum(raw * raw, axis=1, keepdims=True) + 1e-06)
    return raw * inv, inv


def tile_grad(x, y, scale, bias, matching=False):
    logits = scale * product(x, y, NT) + bias
    if matching:
        diag = lax.broadcasted_iota(jnp.int32, logits.shape, 0) == (
            lax.broadcasted_iota(jnp.int32, logits.shape, 1)
        )
        sign = jnp.where(diag, -1.0, 1.0)
        coeff = sign * jax.nn.sigmoid(sign * logits)
    else:
        coeff = jax.nn.sigmoid(logits)
    return product(split(coeff), y, NN)


def unit_kernel(img_in, txt_in, ihat, that, both, ihat_a, ihat_b, *refs):
    (iinv, ihi, ilo, tinv, thi, tlo, raw, sems) = refs
    rows = ihat.shape[0]
    part = rows // PARTS
    copies = []
    for n, source in enumerate((img_in, txt_in)):
        for k in range(PARTS):
            copies.append(
                pltpu.make_async_copy(
                    source.at[pl.ds(k * part, part)],
                    raw.at[pl.ds(n * rows + k * part, part)],
                    sems.at[n, k],
                )
            )
    for copy in copies:
        copy.start()
    for n, (hat, inv, hi, lo) in enumerate(((ihat, iinv, ihi, ilo), (that, tinv, thi, tlo))):
        for copy in copies[n * PARTS : (n + 1) * PARTS]:
            copy.wait()
        hat[...], inv[...] = unit(raw[n * rows : (n + 1) * rows])
        both[n * rows : (n + 1) * rows] = hat[...]
        hi[...], lo[...] = split(hat[...])
        if n == 0:
            ihat_a[...] = hat[: ihat_a.shape[0]]
            ihat_b[...] = hat[ihat_a.shape[0] :]


def own_kernel(scale, bias, ihi, ilo, thi, tlo, igrad, tgrad):
    x, y = (ihi[...], ilo[...]), (thi[...], tlo[...])
    igrad[...] = tile_grad(x, y, scale[0], bias[0], True)
    tgrad[...] = tile_grad(y, x, scale[0], bias[0], True)


def tile_kernel(scale, bias, hi, lo, hat, grad, total):
    total[...] = grad[...] + tile_grad(
        (hi[...], lo[...]), split(hat[...]), scale[0], bias[0]
    )


def raw_kernel(scale, bias, hi, lo, raw, grad, hat, total):
    hat[...] = unit(raw[...])[0]
    tile_kernel(scale, bias, hi, lo, hat, grad, total)


def pair_kernel(scale, bias, ihi, ilo, thi, tlo, both, igrad, tgrad, itotal, ttotal):
    rows = igrad.shape[0]
    tile_kernel(scale, bias, ihi, ilo, both.at[rows:], igrad, itotal)
    tile_kernel(scale, bias, thi, tlo, both.at[:rows], tgrad, ttotal)


def cross_kernel(scale, bias, hi, lo, hat, grad, own, total, inner):
    tile_kernel(scale, bias, hi, lo, hat, grad, total)
    inner[...] = jnp.sum(own[...] * total[...], axis=1, keepdims=True)


def stacked(hi, lo, y_hi, y_lo, scale, bias):
    rows = y_hi.shape[0]
    mul = functools.partial(lax.dot_general, preferred_element_type=F32)
    both = mul(hi, jnp.concatenate([y_hi, y_lo], axis=0), NT)
    dots = both[:, :rows] + (both[:, rows:] + mul(lo, y_hi, NT))
    coeff = jax.nn.sigmoid(scale * dots + bias)
    top, rest = split(coeff)
    left = jnp.concatenate([top, rest], axis=1)
    right = jnp.concatenate([y_hi, y_hi], axis=0)
    return dots, coeff, lambda here: (
        mul(left, right[:, here], NN) + mul(top, y_lo[:, here], NN)
    )


def last_kernel(hats, scale, bias, hi, lo, *refs):
    grad, own, inner, inv, out, part, sems = refs[hats:]
    hat = refs[0][...]
    for more in refs[1:hats]:
        hat += more[...]
    y = split(hat)
    if 2 * hat.shape[0] <= hi.shape[0]:
        dots, coeff, columns = stacked(hi[...], lo[...], *y, scale[0], bias[0])
    else:
        dots = product((hi[...], lo[...]), y, NT)
        coeff = jax.nn.sigmoid(scale[0] * dots + bias[0])
        halves = split(coeff)
        columns = lambda here: product(halves, [half[:, here] for half in y], NN)
    along = inner[...] + jnp.sum(coeff * dots, axis=1, keepdims=True)
    factor = scale[0] * inv[...]
    copies = []
    width = hat.shape[1]
    for at in range(0, width, COLUMNS):
        here = slice(at, min(at + COLUMNS, width))
        total = grad[:, here] + columns(here)
        part[:, here] = (total - own[:, here] * along) * factor
        wide = pl.ds(at, here.stop - at)
        copies.append(
            pltpu.make_async_copy(
                part.at[:, wide], out.at[:, wide], sems.at[at // COLUMNS]
            )
        )
        copies[-1].start()
    for copy in copies:
        copy.wait()


def call(kernel, name, operands, outs, scalars=2, spec=VMEM, out_spec=VMEM, **extra):
    return pl.pallas_call(
        kernel,
        name=name,
        out_shape=outs,
        in_specs=[SMEM] * scalars + [spec] * (len(operands) - scalars),
        out_specs=jax.tree.map(lambda _: out_spec, outs),
        compiler_params=pltpu.CompilerParams(vmem_limit_bytes=24 * 2**20),
        cost_estimate=pl.CostEstimate(
            flops=1 if name in LATE else 2 * 10**10, bytes_accessed=0, transcendentals=0
        ),
        **extra,
    )(*operands)


def body(image_embed, text_embed, logit_scale, logit_bias):
    rows, width = image_embed.shape
    size = lax.axis_size("dp")

    def shape(height, wide=width, kind=F32):
        return jax.ShapeDtypeStruct((height, wide), kind)

    one = shape(rows)
    tail = rows // 2
    column = shape(rows, 1)
    state = (column, shape(rows, kind=BF16), shape(rows, kind=BF16))
    tb = (logit_scale, logit_bias)

    def outward(block):
        return lax.ppermute(
            block, "dp", [(d, (d + (2 if d % 2 else -2)) % size) for d in range(size)]
        )

    def inward(block, skip=()):
        pairs = [(d, (d + (-2 if d % 2 else 2)) % size) for d in range(size)]
        return lax.ppermute(block, "dp", [pair for pair in pairs if pair not in skip])

    seams = range(0, size, SEAM)
    direct = [
        pair
        for at in seams
        for pair in (((at - 2) % size, at), (at + 1, (at - 1) % size))
    ]
    via = [mid for at in seams for mid in ((at + 14) % size, (at - 15) % size)]

    def relay_out(block):
        return lax.ppermute(block, "dp", [(pair[0], mid) for pair, mid in zip(direct, via)])

    def relay_in(block):
        return lax.ppermute(block, "dp", [(mid, pair[1]) for pair, mid in zip(direct, via)])

    def swap(block):
        return lax.ppermute(block, "dp", [(d, d ^ 1) for d in range(size)])

    def last(name, hats, *operands):
        return call(
            functools.partial(last_kernel, hats),
            name,
            (*tb, *operands),
            one,
            out_spec=HBM,
            scratch_shapes=[
                pltpu.VMEM((rows, width), F32),
                pltpu.SemaphoreType.DMA((pl.cdiv(width, COLUMNS),)),
            ],
        )

    def after(*values):
        return lax.optimization_barrier(values)

    near_txt = outward(text_embed)
    in_hbm = [
        pltpu.with_memory_space_constraint(raw, pltpu.HBM)
        for raw in (image_embed, text_embed)
    ]
    ihat, that, both, ihat_a, ihat_b, *rest = call(
        unit_kernel,
        "unit_rows",
        in_hbm,
        (one, one, shape(2 * rows), shape(rows - tail), shape(tail), *state, *state),
        scalars=0,
        spec=HBM,
        scratch_shapes=[
            pltpu.VMEM((2 * rows, width), F32),
            pltpu.SemaphoreType.DMA((2, PARTS)),
        ],
    )
    iinv, ihi, ilo, tinv, thi, tlo = rest
    img, txt = (ihi, ilo), (thi, tlo)
    near_img = outward(ihat)
    pair = swap(both)
    igrad, tgrad = call(own_kernel, "own_tiles", (*tb, *img, *txt), (one, one))

    that_late, igrad, tgrad = after(that, igrad, tgrad)
    far_txt = inward(that_late)
    relayed = relay_out(ihat_b)
    near_txt, igrad = call(
        raw_kernel, "near_text", (*tb, *img, near_txt, igrad), (one, one)
    )
    ihat_a, ihat_b, near_txt, igrad = after(ihat_a, ihat_b, near_txt, igrad)
    far_img_a = inward(ihat_a)
    far_img_b = inward(ihat_b, direct)
    cross_txt = swap(near_txt)
    igrad, tgrad = call(
        pair_kernel, "pair_tiles", (*tb, *img, *txt, pair, igrad, tgrad), (one, one)
    )
    igrad, inner_img = call(
        cross_kernel, "cross_text", (*tb, *img, cross_txt, igrad, ihat), (one, column)
    )

    relayed, igrad = after(relayed, igrad)
    relayed = relay_in(relayed)
    near_img, igrad = after(near_img, igrad)
    cross_img = swap(near_img)
    tgrad = call(tile_kernel, "near_image", (*tb, *txt, near_img, tgrad), one)

    far_txt, igrad, tgrad = after(far_txt, igrad, tgrad)
    grad_image = last("last_text", 1, *img, far_txt, igrad, ihat, inner_img, iinv)
    cross_img, grad_image = after(cross_img, grad_image)
    tgrad = call(tile_kernel, "cross_image", (*tb, *txt, cross_img, tgrad), one)
    tgrad, inner_txt = call(
        cross_kernel, "far_image", (*tb, *txt, far_img_a, tgrad, that), (one, column)
    )
    grad_text = last(
        "last_image", 2, *txt, far_img_b, relayed, tgrad, that, inner_txt, tinv
    )
    return grad_image, grad_text


def solution(mesh):
    return jax.shard_map(
        body,
        mesh=mesh,
        in_specs=(P("dp", None), P("dp", None), P(), P()),
        out_specs=(P("dp", None), P("dp", None)),
        check_vma=False,
    )
```

```python
import functools

import jax
import jax.numpy as jnp
from jax import lax
from jax.experimental import pallas as pl
from jax.experimental.pallas import tpu as pltpu
from jax.sharding import PartitionSpec as P

F32 = jnp.float32
BF16 = jnp.bfloat16
VMEM = pl.BlockSpec(memory_space=pltpu.VMEM)
SMEM = pl.BlockSpec(memory_space=pltpu.SMEM)
HBM = pl.BlockSpec(memory_space=pltpu.HBM)
PARTS = 4
COLUMNS = 256
NT = (((1,), (1,)), ((), ()))
NN = (((1,), (0,)), ((), ()))


def split(value):
    hi = value.astype(BF16)
    return hi, (value - hi.astype(F32)).astype(BF16)


def product(left, right, dims):
    mul = functools.partial(
        lax.dot_general, dimension_numbers=dims, preferred_element_type=F32
    )
    (lh, ll), (rh, rl) = left, right
    return mul(lh, rh) + (mul(lh, rl) + mul(ll, rh))


def unit(raw):
    inv = 1.0 / jnp.sqrt(jnp.sum(raw * raw, axis=1, keepdims=True) + 1e-06)
    return raw * inv, inv


def tile_grad(x, y, scale, bias, matching=False):
    logits = scale * product(x, y, NT) + bias
    if matching:
        diag = lax.broadcasted_iota(jnp.int32, logits.shape, 0) == (
            lax.broadcasted_iota(jnp.int32, logits.shape, 1)
        )
        sign = jnp.where(diag, -1.0, 1.0)
        coeff = sign * jax.nn.sigmoid(sign * logits)
    else:
        coeff = jax.nn.sigmoid(logits)
    return product(split(coeff), y, NN)


def unit_kernel(img_in, txt_in, ihat, that, both, ihat_a, ihat_b, *refs):
    (iinv, ihi, ilo, tinv, thi, tlo, raw, sems) = refs
    rows = ihat.shape[0]
    part = rows // PARTS
    copies = []
    for n, source in enumerate((img_in, txt_in)):
        for k in range(PARTS):
            copies.append(
                pltpu.make_async_copy(
                    source.at[pl.ds(k * part, part)],
                    raw.at[pl.ds(n * rows + k * part, part)],
                    sems.at[n, k],
                )
            )
    for copy in copies:
        copy.start()
    for n, (hat, inv, hi, lo) in enumerate(((ihat, iinv, ihi, ilo), (that, tinv, thi, tlo))):
        for copy in copies[n * PARTS : (n + 1) * PARTS]:
            copy.wait()
        hat[...], inv[...] = unit(raw[n * rows : (n + 1) * rows])
        both[n * rows : (n + 1) * rows] = hat[...]
        hi[...], lo[...] = split(hat[...])
        if n == 0:
            ihat_a[...] = hat[: ihat_a.shape[0]]
            ihat_b[...] = hat[ihat_a.shape[0] :]


def own_kernel(scale, bias, ihi, ilo, thi, tlo, igrad, tgrad):
    x, y = (ihi[...], ilo[...]), (thi[...], tlo[...])
    igrad[...] = tile_grad(x, y, scale[0], bias[0], True)
    tgrad[...] = tile_grad(y, x, scale[0], bias[0], True)


def tile_kernel(scale, bias, hi, lo, hat, grad, total):
    total[...] = grad[...] + tile_grad(
        (hi[...], lo[...]), split(hat[...]), scale[0], bias[0]
    )


def raw_kernel(scale, bias, hi, lo, raw, grad, hat, total):
    hat[...] = unit(raw[...])[0]
    tile_kernel(scale, bias, hi, lo, hat, grad, total)


def pair_kernel(scale, bias, ihi, ilo, thi, tlo, both, igrad, tgrad, itotal, ttotal):
    rows = igrad.shape[0]
    tile_kernel(scale, bias, ihi, ilo, both.at[rows:], igrad, itotal)
    tile_kernel(scale, bias, thi, tlo, both.at[:rows], tgrad, ttotal)


def cross_kernel(scale, bias, hi, lo, hat, grad, own, total, inner):
    tile_kernel(scale, bias, hi, lo, hat, grad, total)
    inner[...] = jnp.sum(own[...] * total[...], axis=1, keepdims=True)


def stacked(hi, lo, y_hi, y_lo, scale, bias):
    rows = y_hi.shape[0]
    mul = functools.partial(lax.dot_general, preferred_element_type=F32)
    both = mul(hi, jnp.concatenate([y_hi, y_lo], axis=0), NT)
    dots = both[:, :rows] + (both[:, rows:] + mul(lo, y_hi, NT))
    coeff = jax.nn.sigmoid(scale * dots + bias)
    top, rest = split(coeff)
    left = jnp.concatenate([top, rest], axis=1)
    right = jnp.concatenate([y_hi, y_hi], axis=0)
    return dots, coeff, lambda here: (
        mul(left, right[:, here], NN) + mul(top, y_lo[:, here], NN)
    )


def last_kernel(scale, bias, hi, lo, hat, grad, own, inner, inv, out, part, sems):
    y = split(hat[...])
    if 2 * hat.shape[0] <= hi.shape[0]:
        dots, coeff, columns = stacked(hi[...], lo[...], *y, scale[0], bias[0])
    else:
        dots = product((hi[...], lo[...]), y, NT)
        coeff = jax.nn.sigmoid(scale[0] * dots + bias[0])
        halves = split(coeff)
        columns = lambda here: product(halves, [half[:, here] for half in y], NN)
    along = inner[...] + jnp.sum(coeff * dots, axis=1, keepdims=True)
    factor = scale[0] * inv[...]
    copies = []
    width = hat.shape[1]
    for at in range(0, width, COLUMNS):
        here = slice(at, min(at + COLUMNS, width))
        total = grad[:, here] + columns(here)
        part[:, here] = (total - own[:, here] * along) * factor
        wide = pl.ds(at, here.stop - at)
        copies.append(
            pltpu.make_async_copy(
                part.at[:, wide], out.at[:, wide], sems.at[at // COLUMNS]
            )
        )
        copies[-1].start()
    for copy in copies:
        copy.wait()


def call(kernel, name, operands, outs, scalars=2, spec=VMEM, out_spec=VMEM, **extra):
    return pl.pallas_call(
        kernel,
        name=name,
        out_shape=outs,
        in_specs=[SMEM] * scalars + [spec] * (len(operands) - scalars),
        out_specs=jax.tree.map(lambda _: out_spec, outs),
        compiler_params=pltpu.CompilerParams(vmem_limit_bytes=24 * 2**20),
        cost_estimate=pl.CostEstimate(flops=2 * 10**10, bytes_accessed=0, transcendentals=0),
        **extra,
    )(*operands)


def body(image_embed, text_embed, logit_scale, logit_bias):
    rows, width = image_embed.shape
    size = lax.axis_size("dp")

    def shape(height, wide=width, kind=F32):
        return jax.ShapeDtypeStruct((height, wide), kind)

    one = shape(rows)
    tail = rows // 2
    column = shape(rows, 1)
    state = (column, shape(rows, kind=BF16), shape(rows, kind=BF16))
    tb = (logit_scale, logit_bias)

    def outward(block):
        return lax.ppermute(
            block, "dp", [(d, (d + (2 if d % 2 else -2)) % size) for d in range(size)]
        )

    def inward(block):
        return lax.ppermute(
            block, "dp", [(d, (d + (-2 if d % 2 else 2)) % size) for d in range(size)]
        )

    def swap(block):
        return lax.ppermute(block, "dp", [(d, d ^ 1) for d in range(size)])

    def last(name, *operands):
        return call(
            last_kernel,
            name,
            (*tb, *operands),
            one,
            out_spec=HBM,
            scratch_shapes=[
                pltpu.VMEM((rows, width), F32),
                pltpu.SemaphoreType.DMA((pl.cdiv(width, COLUMNS),)),
            ],
        )

    def after(*values):
        return lax.optimization_barrier(values)

    near_txt = outward(text_embed)
    in_hbm = [
        pltpu.with_memory_space_constraint(raw, pltpu.HBM)
        for raw in (image_embed, text_embed)
    ]
    ihat, that, both, ihat_a, ihat_b, *rest = call(
        unit_kernel,
        "unit_rows",
        in_hbm,
        (one, one, shape(2 * rows), shape(rows - tail), shape(tail), *state, *state),
        scalars=0,
        spec=HBM,
        scratch_shapes=[
            pltpu.VMEM((2 * rows, width), F32),
            pltpu.SemaphoreType.DMA((2, PARTS)),
        ],
    )
    iinv, ihi, ilo, tinv, thi, tlo = rest
    img, txt = (ihi, ilo), (thi, tlo)
    near_img = outward(ihat)
    pair = swap(both)
    igrad, tgrad = call(own_kernel, "own_tiles", (*tb, *img, *txt), (one, one))

    that_late, igrad, tgrad = after(that, igrad, tgrad)
    far_txt = inward(that_late)
    near_txt, igrad = call(
        raw_kernel, "near_text", (*tb, *img, near_txt, igrad), (one, one)
    )
    ihat_a, ihat_b, near_txt, igrad = after(ihat_a, ihat_b, near_txt, igrad)
    far_img_a = inward(ihat_a)
    far_img_b = inward(ihat_b)
    cross_txt = swap(near_txt)
    igrad, tgrad = call(
        pair_kernel, "pair_tiles", (*tb, *img, *txt, pair, igrad, tgrad), (one, one)
    )
    igrad, inner_img = call(
        cross_kernel, "cross_text", (*tb, *img, cross_txt, igrad, ihat), (one, column)
    )

    near_img, igrad = after(near_img, igrad)
    cross_img = swap(near_img)
    tgrad = call(tile_kernel, "near_image", (*tb, *txt, near_img, tgrad), one)

    far_txt, igrad, tgrad = after(far_txt, igrad, tgrad)
    grad_image = last("last_text", *img, far_txt, igrad, ihat, inner_img, iinv)
    cross_img, grad_image = after(cross_img, grad_image)
    tgrad = call(tile_kernel, "cross_image", (*tb, *txt, cross_img, tgrad), one)
    tgrad, inner_txt = call(
        cross_kernel, "far_image", (*tb, *txt, far_img_a, tgrad, that), (one, column)
    )
    grad_text = last("last_image", *txt, far_img_b, tgrad, that, inner_txt, tinv)
    return grad_image, grad_text


def solution(mesh):
    return jax.shard_map(
        body,
        mesh=mesh,
        in_specs=(P("dp", None), P("dp", None), P(), P()),
        out_specs=(P("dp", None), P("dp", None)),
        check_vma=False,
    )
```

```python
import functools

import jax
import jax.numpy as jnp
from jax import lax
from jax.experimental import pallas as pl
from jax.experimental.pallas import tpu as pltpu
from jax.sharding import PartitionSpec as P

F32 = jnp.float32
BF16 = jnp.bfloat16
VMEM = pl.BlockSpec(memory_space=pltpu.VMEM)
SMEM = pl.BlockSpec(memory_space=pltpu.SMEM)
HBM = pl.BlockSpec(memory_space=pltpu.HBM)
PARTS = 4
COLUMNS = 256
SEAM = 128
HINTS = {"near_text": 4 * 10**10, "last_text": 1, "cross_image": 1, "far_image": 1}
NT = (((1,), (1,)), ((), ()))
NN = (((1,), (0,)), ((), ()))


def split(value):
    hi = value.astype(BF16)
    return hi, (value - hi.astype(F32)).astype(BF16)


def product(left, right, dims):
    mul = functools.partial(
        lax.dot_general, dimension_numbers=dims, preferred_element_type=F32
    )
    (lh, ll), (rh, rl) = left, right
    return mul(lh, rh) + (mul(lh, rl) + mul(ll, rh))


def unit(raw):
    inv = 1.0 / jnp.sqrt(jnp.sum(raw * raw, axis=1, keepdims=True) + 1e-06)
    return raw * inv, inv


def tile_grad(x, y, scale, bias, matching=False):
    logits = scale * product(x, y, NT) + bias
    if matching:
        diag = lax.broadcasted_iota(jnp.int32, logits.shape, 0) == (
            lax.broadcasted_iota(jnp.int32, logits.shape, 1)
        )
        sign = jnp.where(diag, -1.0, 1.0)
        coeff = sign * jax.nn.sigmoid(sign * logits)
    else:
        coeff = jax.nn.sigmoid(logits)
    return product(split(coeff), y, NN)


def unit_kernel(img_in, txt_in, ihat, that, both, ihat_a, ihat_b, *refs):
    (iinv, ihi, ilo, tinv, thi, tlo, raw, sems) = refs
    rows = ihat.shape[0]
    part = rows // PARTS
    copies = []
    for n, source in enumerate((img_in, txt_in)):
        for k in range(PARTS):
            copies.append(
                pltpu.make_async_copy(
                    source.at[pl.ds(k * part, part)],
                    raw.at[pl.ds(n * rows + k * part, part)],
                    sems.at[n, k],
                )
            )
    for copy in copies:
        copy.start()
    for n, (hat, inv, hi, lo) in enumerate(((ihat, iinv, ihi, ilo), (that, tinv, thi, tlo))):
        for copy in copies[n * PARTS : (n + 1) * PARTS]:
            copy.wait()
        hat[...], inv[...] = unit(raw[n * rows : (n + 1) * rows])
        both[n * rows : (n + 1) * rows] = hat[...]
        hi[...], lo[...] = split(hat[...])
        if n == 0:
            ihat_a[...] = hat[: ihat_a.shape[0]]
            ihat_b[...] = hat[ihat_a.shape[0] :]


def own_kernel(scale, bias, ihi, ilo, thi, tlo, igrad, tgrad):
    x, y = (ihi[...], ilo[...]), (thi[...], tlo[...])
    igrad[...] = tile_grad(x, y, scale[0], bias[0], True)
    tgrad[...] = tile_grad(y, x, scale[0], bias[0], True)


def tile_kernel(scale, bias, hi, lo, hat, grad, total):
    total[...] = grad[...] + tile_grad(
        (hi[...], lo[...]), split(hat[...]), scale[0], bias[0]
    )


def near_kernel(shared_in, raw, shared, hat):
    del shared_in
    hat[...] = unit(raw[...])[0]
    shared[2 * raw.shape[0] :] = hat[...]


def pair_kernel(scale, bias, ihi, ilo, thi, tlo, shared, igrad, tgrad, own, *outs):
    itotal, ttotal, inner, passed = outs
    rows = igrad.shape[0]
    tile_kernel(scale, bias, thi, tlo, shared.at[:rows], tgrad, ttotal)
    passed[...] = shared[rows - passed.shape[0] : rows]
    tile_kernel(scale, bias, ihi, ilo, shared.at[rows : 2 * rows], igrad, itotal)
    cross_kernel(scale, bias, ihi, ilo, shared.at[2 * rows :], itotal, own, itotal, inner)


def cross_kernel(scale, bias, hi, lo, hat, grad, own, total, inner):
    tile_kernel(scale, bias, hi, lo, hat, grad, total)
    inner[...] = jnp.sum(own[...] * total[...], axis=1, keepdims=True)


def stacked(hi, lo, y_hi, y_lo, scale, bias):
    rows = y_hi.shape[0]
    mul = functools.partial(lax.dot_general, preferred_element_type=F32)
    both = mul(hi, jnp.concatenate([y_hi, y_lo], axis=0), NT)
    dots = both[:, :rows] + (both[:, rows:] + mul(lo, y_hi, NT))
    coeff = jax.nn.sigmoid(scale * dots + bias)
    top, rest = split(coeff)
    left = jnp.concatenate([top, rest], axis=1)
    right = jnp.concatenate([y_hi, y_hi], axis=0)
    return dots, coeff, lambda here: (
        mul(left, right[:, here], NN) + mul(top, y_lo[:, here], NN)
    )


def last_kernel(hats, scale, bias, hi, lo, *refs):
    grad, own, inner, inv, out, part, sems = refs[hats:]
    hat = refs[0][...]
    for more in refs[1:hats]:
        hat += more[...]
    y = split(hat)
    if 2 * hat.shape[0] <= hi.shape[0]:
        dots, coeff, columns = stacked(hi[...], lo[...], *y, scale[0], bias[0])
    else:
        dots = product((hi[...], lo[...]), y, NT)
        coeff = jax.nn.sigmoid(scale[0] * dots + bias[0])
        halves = split(coeff)
        columns = lambda here: product(halves, [half[:, here] for half in y], NN)
    along = inner[...] + jnp.sum(coeff * dots, axis=1, keepdims=True)
    factor = scale[0] * inv[...]
    copies = []
    width = hat.shape[1]
    for at in range(0, width, COLUMNS):
        here = slice(at, min(at + COLUMNS, width))
        total = grad[:, here] + columns(here)
        part[:, here] = (total - own[:, here] * along) * factor
        wide = pl.ds(at, here.stop - at)
        copies.append(
            pltpu.make_async_copy(
                part.at[:, wide], out.at[:, wide], sems.at[at // COLUMNS]
            )
        )
        copies[-1].start()
    for copy in copies:
        copy.wait()


def call(kernel, name, operands, outs, scalars=2, spec=VMEM, out_spec=VMEM, **extra):
    return pl.pallas_call(
        kernel,
        name=name,
        out_shape=outs,
        in_specs=[SMEM] * scalars + [spec] * (len(operands) - scalars),
        out_specs=jax.tree.map(lambda _: out_spec, outs),
        compiler_params=pltpu.CompilerParams(vmem_limit_bytes=24 * 2**20),
        cost_estimate=pl.CostEstimate(
            flops=HINTS.get(name, 2 * 10**10), bytes_accessed=0, transcendentals=0
        ),
        **extra,
    )(*operands)


def body(image_embed, text_embed, logit_scale, logit_bias):
    rows, width = image_embed.shape
    size = lax.axis_size("dp")

    def shape(height, wide=width, kind=F32):
        return jax.ShapeDtypeStruct((height, wide), kind)

    one = shape(rows)
    tail = rows // 2
    column = shape(rows, 1)
    state = (column, shape(rows, kind=BF16), shape(rows, kind=BF16))
    tb = (logit_scale, logit_bias)

    def outward(block):
        return lax.ppermute(
            block, "dp", [(d, (d + (2 if d % 2 else -2)) % size) for d in range(size)]
        )

    def inward(block, skip=()):
        pairs = [(d, (d + (-2 if d % 2 else 2)) % size) for d in range(size)]
        return lax.ppermute(block, "dp", [pair for pair in pairs if pair not in skip])

    seams = range(0, size, SEAM)
    handed_over = [(at + 1, (at - 1) % size) for at in seams]

    def instead(block):
        return lax.ppermute(block, "dp", [(d - 1, to) for d, to in handed_over])

    def swap(block):
        return lax.ppermute(block, "dp", [(d, d ^ 1) for d in range(size)])

    def last(name, hats, *operands):
        return call(
            functools.partial(last_kernel, hats),
            name,
            (*tb, *operands),
            one,
            out_spec=HBM,
            scratch_shapes=[
                pltpu.VMEM((rows, width), F32),
                pltpu.SemaphoreType.DMA((pl.cdiv(width, COLUMNS),)),
            ],
        )

    def after(*values):
        return lax.optimization_barrier(values)

    near_txt = outward(text_embed)
    in_hbm = [
        pltpu.with_memory_space_constraint(raw, pltpu.HBM)
        for raw in (image_embed, text_embed)
    ]
    ihat, that, both, ihat_a, ihat_b, *rest = call(
        unit_kernel,
        "unit_rows",
        in_hbm,
        (one, one, shape(3 * rows), shape(rows - tail), shape(tail), *state, *state),
        scalars=0,
        spec=HBM,
        scratch_shapes=[
            pltpu.VMEM((2 * rows, width), F32),
            pltpu.SemaphoreType.DMA((2, PARTS)),
        ],
    )
    iinv, ihi, ilo, tinv, thi, tlo = rest
    img, txt = (ihi, ilo), (thi, tlo)
    near_img = outward(ihat)
    igrad, tgrad = call(own_kernel, "own_tiles", (*tb, *img, *txt), (one, one))

    near_txt, igrad, tgrad = after(near_txt, igrad, tgrad)
    both, near_txt = call(
        near_kernel,
        "near_rows",
        (both, near_txt),
        (shape(3 * rows), one),
        scalars=0,
        input_output_aliases={0: 0},
    )
    that_late, near_txt = after(that, near_txt)
    far_txt = inward(that_late)
    pair = swap(both)
    igrad = call(tile_kernel, "near_text", (*tb, *img, near_txt, igrad), one)
    ihat_a, ihat_b, igrad = after(ihat_a, ihat_b, igrad)
    far_img_a = inward(ihat_a)
    far_img_b = inward(ihat_b, handed_over)
    igrad, tgrad, inner_img, passed = call(
        pair_kernel,
        "pair_tiles",
        (*tb, *img, *txt, pair, igrad, tgrad, ihat),
        (one, one, column, shape(tail)),
    )
    far_img_c = instead(passed)

    near_img, igrad = after(near_img, igrad)
    cross_img = swap(near_img)
    tgrad = call(tile_kernel, "near_image", (*tb, *txt, near_img, tgrad), one)

    far_txt, igrad, tgrad = after(far_txt, igrad, tgrad)
    grad_image = last("last_text", 1, *img, far_txt, igrad, ihat, inner_img, iinv)
    cross_img, grad_image = after(cross_img, grad_image)
    tgrad = call(tile_kernel, "cross_image", (*tb, *txt, cross_img, tgrad), one)
    tgrad, inner_txt = call(
        cross_kernel, "far_image", (*tb, *txt, far_img_a, tgrad, that), (one, column)
    )
    grad_text = last(
        "last_image", 2, *txt, far_img_b, far_img_c, tgrad, that, inner_txt, tinv
    )
    return grad_image, grad_text


def solution(mesh):
    return jax.shard_map(
        body,
        mesh=mesh,
        in_specs=(P("dp", None), P("dp", None), P(), P()),
        out_specs=(P("dp", None), P("dp", None)),
        check_vma=False,
    )
```

```python
import functools

import jax
import jax.numpy as jnp
from jax import lax
from jax.experimental import pallas as pl
from jax.experimental.pallas import tpu as pltpu
from jax.sharding import PartitionSpec as P

F32 = jnp.float32
BF16 = jnp.bfloat16
VMEM = pl.BlockSpec(memory_space=pltpu.VMEM)
SMEM = pl.BlockSpec(memory_space=pltpu.SMEM)
HBM = pl.BlockSpec(memory_space=pltpu.HBM)
PARTS = 4
COLUMNS = 256
HINTS = {"last_text": 1, "cross_image": 1, "far_image": 1}
NT = (((1,), (1,)), ((), ()))
NN = (((1,), (0,)), ((), ()))


def split(value):
    hi = value.astype(BF16)
    return hi, (value - hi.astype(F32)).astype(BF16)


def product(left, right, dims):
    mul = functools.partial(
        lax.dot_general, dimension_numbers=dims, preferred_element_type=F32
    )
    (lh, ll), (rh, rl) = left, right
    return mul(lh, rh) + (mul(lh, rl) + mul(ll, rh))


def unit(raw):
    inv = 1.0 / jnp.sqrt(jnp.sum(raw * raw, axis=1, keepdims=True) + 1e-06)
    return raw * inv, inv


def tile_grad(x, y, scale, bias, matching=False):
    logits = scale * product(x, y, NT) + bias
    if matching:
        diag = lax.broadcasted_iota(jnp.int32, logits.shape, 0) == (
            lax.broadcasted_iota(jnp.int32, logits.shape, 1)
        )
        sign = jnp.where(diag, -1.0, 1.0)
        coeff = sign * jax.nn.sigmoid(sign * logits)
    else:
        coeff = jax.nn.sigmoid(logits)
    return product(split(coeff), y, NN)


def unit_kernel(img_in, txt_in, ihat, that, both, ihat_a, ihat_b, *refs):
    (iinv, ihi, ilo, tinv, thi, tlo, raw, sems) = refs
    rows = ihat.shape[0]
    part = rows // PARTS
    copies = []
    for n, source in enumerate((img_in, txt_in)):
        for k in range(PARTS):
            copies.append(
                pltpu.make_async_copy(
                    source.at[pl.ds(k * part, part)],
                    raw.at[pl.ds(n * rows + k * part, part)],
                    sems.at[n, k],
                )
            )
    for copy in copies:
        copy.start()
    for n, (hat, inv, hi, lo) in enumerate(((ihat, iinv, ihi, ilo), (that, tinv, thi, tlo))):
        for copy in copies[n * PARTS : (n + 1) * PARTS]:
            copy.wait()
        hat[...], inv[...] = unit(raw[n * rows : (n + 1) * rows])
        both[n * rows : (n + 1) * rows] = hat[...]
        hi[...], lo[...] = split(hat[...])
        if n == 0:
            ihat_a[...] = hat[: ihat_a.shape[0]]
            ihat_b[...] = hat[ihat_a.shape[0] :]


def own_kernel(scale, bias, ihi, ilo, thi, tlo, igrad, tgrad):
    x, y = (ihi[...], ilo[...]), (thi[...], tlo[...])
    igrad[...] = tile_grad(x, y, scale[0], bias[0], True)
    tgrad[...] = tile_grad(y, x, scale[0], bias[0], True)


def tile_kernel(scale, bias, hi, lo, hat, grad, total):
    total[...] = grad[...] + tile_grad(
        (hi[...], lo[...]), split(hat[...]), scale[0], bias[0]
    )


def raw_kernel(scale, bias, hi, lo, raw, grad, hat, total):
    hat[...] = unit(raw[...])[0]
    tile_kernel(scale, bias, hi, lo, hat, grad, total)


def pair_kernel(scale, bias, ihi, ilo, thi, tlo, both, igrad, tgrad, *outs):
    itotal, ttotal, passed = outs
    rows = igrad.shape[0]
    passed[...] = both[rows - passed.shape[0] : rows]
    tile_kernel(scale, bias, ihi, ilo, both.at[rows:], igrad, itotal)
    tile_kernel(scale, bias, thi, tlo, both.at[:rows], tgrad, ttotal)


def cross_kernel(scale, bias, hi, lo, hat, grad, own, total, inner):
    tile_kernel(scale, bias, hi, lo, hat, grad, total)
    inner[...] = jnp.sum(own[...] * total[...], axis=1, keepdims=True)


def stacked(hi, lo, y_hi, y_lo, scale, bias):
    rows = y_hi.shape[0]
    mul = functools.partial(lax.dot_general, preferred_element_type=F32)
    both = mul(hi, jnp.concatenate([y_hi, y_lo], axis=0), NT)
    dots = both[:, :rows] + (both[:, rows:] + mul(lo, y_hi, NT))
    coeff = jax.nn.sigmoid(scale * dots + bias)
    top, rest = split(coeff)
    left = jnp.concatenate([top, rest], axis=1)
    right = jnp.concatenate([y_hi, y_hi], axis=0)
    return dots, coeff, lambda here: (
        mul(left, right[:, here], NN) + mul(top, y_lo[:, here], NN)
    )


def last_kernel(hats, scale, bias, hi, lo, *refs):
    grad, own, inner, inv, out, part, sems = refs[hats:]
    hat = refs[0][...]
    for more in refs[1:hats]:
        hat += more[...]
    y = split(hat)
    if 2 * hat.shape[0] <= hi.shape[0]:
        dots, coeff, columns = stacked(hi[...], lo[...], *y, scale[0], bias[0])
    else:
        dots = product((hi[...], lo[...]), y, NT)
        coeff = jax.nn.sigmoid(scale[0] * dots + bias[0])
        halves = split(coeff)
        columns = lambda here: product(halves, [half[:, here] for half in y], NN)
    along = inner[...] + jnp.sum(coeff * dots, axis=1, keepdims=True)
    factor = scale[0] * inv[...]
    copies = []
    width = hat.shape[1]
    for at in range(0, width, COLUMNS):
        here = slice(at, min(at + COLUMNS, width))
        total = grad[:, here] + columns(here)
        part[:, here] = (total - own[:, here] * along) * factor
        wide = pl.ds(at, here.stop - at)
        copies.append(
            pltpu.make_async_copy(
                part.at[:, wide], out.at[:, wide], sems.at[at // COLUMNS]
            )
        )
        copies[-1].start()
    for copy in copies:
        copy.wait()


def call(kernel, name, operands, outs, scalars=2, spec=VMEM, out_spec=VMEM, **extra):
    return pl.pallas_call(
        kernel,
        name=name,
        out_shape=outs,
        in_specs=[SMEM] * scalars + [spec] * (len(operands) - scalars),
        out_specs=jax.tree.map(lambda _: out_spec, outs),
        compiler_params=pltpu.CompilerParams(vmem_limit_bytes=24 * 2**20),
        cost_estimate=pl.CostEstimate(
            flops=HINTS.get(name, 2 * 10**10), bytes_accessed=0, transcendentals=0
        ),
        **extra,
    )(*operands)


def body(image_embed, text_embed, logit_scale, logit_bias):
    rows, width = image_embed.shape
    size = lax.axis_size("dp")

    def shape(height, wide=width, kind=F32):
        return jax.ShapeDtypeStruct((height, wide), kind)

    one = shape(rows)
    tail = rows // 2
    column = shape(rows, 1)
    state = (column, shape(rows, kind=BF16), shape(rows, kind=BF16))
    tb = (logit_scale, logit_bias)

    def outward(block):
        return lax.ppermute(
            block, "dp", [(d, (d + (2 if d % 2 else -2)) % size) for d in range(size)]
        )

    def inward(block, skip=()):
        pairs = [(d, (d + (-2 if d % 2 else 2)) % size) for d in range(size)]
        return lax.ppermute(block, "dp", [pair for pair in pairs if pair not in skip])

    def swap(block):
        return lax.ppermute(block, "dp", [(d, d ^ 1) for d in range(size)])

    def last(name, hats, *operands):
        return call(
            functools.partial(last_kernel, hats),
            name,
            (*tb, *operands),
            one,
            out_spec=HBM,
            scratch_shapes=[
                pltpu.VMEM((rows, width), F32),
                pltpu.SemaphoreType.DMA((pl.cdiv(width, COLUMNS),)),
            ],
        )

    def after(*values):
        return lax.optimization_barrier(values)

    near_txt = outward(text_embed)
    in_hbm = [
        pltpu.with_memory_space_constraint(raw, pltpu.HBM)
        for raw in (image_embed, text_embed)
    ]
    ihat, that, both, ihat_a, ihat_b, *rest = call(
        unit_kernel,
        "unit_rows",
        in_hbm,
        (one, one, shape(2 * rows), shape(rows - tail), shape(tail), *state, *state),
        scalars=0,
        spec=HBM,
        scratch_shapes=[
            pltpu.VMEM((2 * rows, width), F32),
            pltpu.SemaphoreType.DMA((2, PARTS)),
        ],
    )
    iinv, ihi, ilo, tinv, thi, tlo = rest
    img, txt = (ihi, ilo), (thi, tlo)
    near_img = outward(ihat)
    pair = swap(both)
    igrad, tgrad = call(own_kernel, "own_tiles", (*tb, *img, *txt), (one, one))

    that_late, igrad, tgrad = after(that, igrad, tgrad)
    far_txt = inward(that_late)
    near_txt, igrad = call(
        raw_kernel, "near_text", (*tb, *img, near_txt, igrad), (one, one)
    )
    ihat_a, ihat_b, near_txt, igrad = after(ihat_a, ihat_b, near_txt, igrad)
    far_img_a = inward(ihat_a)
    far_img_b = inward(ihat_b, [(1, size - 1)])
    cross_txt = swap(near_txt)
    igrad, tgrad, passed = call(
        pair_kernel,
        "pair_tiles",
        (*tb, *img, *txt, pair, igrad, tgrad),
        (one, one, shape(tail)),
    )
    far_img_c = lax.ppermute(passed, "dp", [(0, size - 1)])
    igrad, inner_img = call(
        cross_kernel, "cross_text", (*tb, *img, cross_txt, igrad, ihat), (one, column)
    )

    near_img, igrad = after(near_img, igrad)
    cross_img = swap(near_img)
    tgrad = call(tile_kernel, "near_image", (*tb, *txt, near_img, tgrad), one)

    far_txt, igrad, tgrad = after(far_txt, igrad, tgrad)
    grad_image = last("last_text", 1, *img, far_txt, igrad, ihat, inner_img, iinv)
    cross_img, grad_image = after(cross_img, grad_image)
    tgrad = call(tile_kernel, "cross_image", (*tb, *txt, cross_img, tgrad), one)
    tgrad, inner_txt = call(
        cross_kernel, "far_image", (*tb, *txt, far_img_a, tgrad, that), (one, column)
    )
    grad_text = last(
        "last_image", 2, *txt, far_img_b, far_img_c, tgrad, that, inner_txt, tinv
    )
    return grad_image, grad_text


def solution(mesh):
    return jax.shard_map(
        body,
        mesh=mesh,
        in_specs=(P("dp", None), P("dp", None), P(), P()),
        out_specs=(P("dp", None), P("dp", None)),
        check_vma=False,
    )
```

```python
import functools

import jax
import jax.numpy as jnp
from jax import lax
from jax.experimental import pallas as pl
from jax.experimental.pallas import tpu as pltpu
from jax.sharding import PartitionSpec as P

F32 = jnp.float32
BF16 = jnp.bfloat16
VMEM = pl.BlockSpec(memory_space=pltpu.VMEM)
SMEM = pl.BlockSpec(memory_space=pltpu.SMEM)
HBM = pl.BlockSpec(memory_space=pltpu.HBM)
PARTS = 4
COLUMNS = 256
SEAM = 128
NT = (((1,), (1,)), ((), ()))
NN = (((1,), (0,)), ((), ()))


def split(value):
    hi = value.astype(BF16)
    return hi, (value - hi.astype(F32)).astype(BF16)


def product(left, right, dims):
    mul = functools.partial(
        lax.dot_general, dimension_numbers=dims, preferred_element_type=F32
    )
    (lh, ll), (rh, rl) = left, right
    return mul(lh, rh) + (mul(lh, rl) + mul(ll, rh))


def unit(raw):
    inv = 1.0 / jnp.sqrt(jnp.sum(raw * raw, axis=1, keepdims=True) + 1e-06)
    return raw * inv, inv


def tile_grad(x, y, scale, bias, matching=False):
    logits = scale * product(x, y, NT) + bias
    if matching:
        diag = lax.broadcasted_iota(jnp.int32, logits.shape, 0) == (
            lax.broadcasted_iota(jnp.int32, logits.shape, 1)
        )
        sign = jnp.where(diag, -1.0, 1.0)
        coeff = sign * jax.nn.sigmoid(sign * logits)
    else:
        coeff = jax.nn.sigmoid(logits)
    return product(split(coeff), y, NN)


def unit_kernel(img_in, txt_in, ihat, that, both, ihat_a, ihat_b, *refs):
    (iinv, ihi, ilo, tinv, thi, tlo, raw, sems) = refs
    rows = ihat.shape[0]
    part = rows // PARTS
    copies = []
    for n, source in enumerate((img_in, txt_in)):
        for k in range(PARTS):
            copies.append(
                pltpu.make_async_copy(
                    source.at[pl.ds(k * part, part)],
                    raw.at[pl.ds(n * rows + k * part, part)],
                    sems.at[n, k],
                )
            )
    for copy in copies:
        copy.start()
    for n, (hat, inv, hi, lo) in enumerate(((ihat, iinv, ihi, ilo), (that, tinv, thi, tlo))):
        for copy in copies[n * PARTS : (n + 1) * PARTS]:
            copy.wait()
        hat[...], inv[...] = unit(raw[n * rows : (n + 1) * rows])
        both[n * rows : (n + 1) * rows] = hat[...]
        hi[...], lo[...] = split(hat[...])
        if n == 0:
            ihat_a[...] = hat[: ihat_a.shape[0]]
            ihat_b[...] = hat[ihat_a.shape[0] :]


def own_kernel(scale, bias, ihi, ilo, thi, tlo, igrad, tgrad):
    x, y = (ihi[...], ilo[...]), (thi[...], tlo[...])
    igrad[...] = tile_grad(x, y, scale[0], bias[0], True)
    tgrad[...] = tile_grad(y, x, scale[0], bias[0], True)


def tile_kernel(scale, bias, hi, lo, hat, grad, total):
    total[...] = grad[...] + tile_grad(
        (hi[...], lo[...]), split(hat[...]), scale[0], bias[0]
    )


def raw_kernel(scale, bias, hi, lo, raw, grad, hat, total):
    hat[...] = unit(raw[...])[0]
    tile_kernel(scale, bias, hi, lo, hat, grad, total)


def choose_kernel(first, both, own_a, own_b, out_a, out_b):
    cut = own_a.shape[0]

    @pl.when(first[0] != 0)
    def _():
        out_a[...] = both[:cut]
        out_b[...] = both[cut : cut + own_b.shape[0]]

    @pl.when(first[0] == 0)
    def _():
        out_a[...] = own_a[...]
        out_b[...] = own_b[...]


def pair_kernel(scale, bias, ihi, ilo, thi, tlo, both, igrad, tgrad, itotal, ttotal):
    rows = igrad.shape[0]
    tile_kernel(scale, bias, ihi, ilo, both.at[rows:], igrad, itotal)
    tile_kernel(scale, bias, thi, tlo, both.at[:rows], tgrad, ttotal)


def cross_kernel(scale, bias, hi, lo, hat, grad, own, total, inner):
    tile_kernel(scale, bias, hi, lo, hat, grad, total)
    inner[...] = jnp.sum(own[...] * total[...], axis=1, keepdims=True)


def stacked(hi, lo, y_hi, y_lo, scale, bias):
    rows = y_hi.shape[0]
    mul = functools.partial(lax.dot_general, preferred_element_type=F32)
    both = mul(hi, jnp.concatenate([y_hi, y_lo], axis=0), NT)
    dots = both[:, :rows] + (both[:, rows:] + mul(lo, y_hi, NT))
    coeff = jax.nn.sigmoid(scale * dots + bias)
    top, rest = split(coeff)
    left = jnp.concatenate([top, rest], axis=1)
    right = jnp.concatenate([y_hi, y_hi], axis=0)
    return dots, coeff, lambda here: (
        mul(left, right[:, here], NN) + mul(top, y_lo[:, here], NN)
    )


def last_kernel(scale, bias, hi, lo, hat, grad, own, inner, inv, out, part, sems):
    y = split(hat[...])
    if 2 * hat.shape[0] <= hi.shape[0]:
        dots, coeff, columns = stacked(hi[...], lo[...], *y, scale[0], bias[0])
    else:
        dots = product((hi[...], lo[...]), y, NT)
        coeff = jax.nn.sigmoid(scale[0] * dots + bias[0])
        halves = split(coeff)
        columns = lambda here: product(halves, [half[:, here] for half in y], NN)
    along = inner[...] + jnp.sum(coeff * dots, axis=1, keepdims=True)
    factor = scale[0] * inv[...]
    copies = []
    width = hat.shape[1]
    for at in range(0, width, COLUMNS):
        here = slice(at, min(at + COLUMNS, width))
        total = grad[:, here] + columns(here)
        part[:, here] = (total - own[:, here] * along) * factor
        wide = pl.ds(at, here.stop - at)
        copies.append(
            pltpu.make_async_copy(
                part.at[:, wide], out.at[:, wide], sems.at[at // COLUMNS]
            )
        )
        copies[-1].start()
    for copy in copies:
        copy.wait()


def call(kernel, name, operands, outs, scalars=2, spec=VMEM, out_spec=VMEM, **extra):
    return pl.pallas_call(
        kernel,
        name=name,
        out_shape=outs,
        in_specs=[SMEM] * scalars + [spec] * (len(operands) - scalars),
        out_specs=jax.tree.map(lambda _: out_spec, outs),
        compiler_params=pltpu.CompilerParams(vmem_limit_bytes=24 * 2**20),
        cost_estimate=pl.CostEstimate(flops=2 * 10**10, bytes_accessed=0, transcendentals=0),
        **extra,
    )(*operands)


def body(image_embed, text_embed, logit_scale, logit_bias):
    rows, width = image_embed.shape
    size = lax.axis_size("dp")

    def shape(height, wide=width, kind=F32):
        return jax.ShapeDtypeStruct((height, wide), kind)

    one = shape(rows)
    tail = rows // 2
    column = shape(rows, 1)
    state = (column, shape(rows, kind=BF16), shape(rows, kind=BF16))
    tb = (logit_scale, logit_bias)

    def outward(block):
        return lax.ppermute(
            block, "dp", [(d, (d + (2 if d % 2 else -2)) % size) for d in range(size)]
        )

    def inward(block):
        return lax.ppermute(
            block, "dp", [(d, (d + (-2 if d % 2 else 2)) % size) for d in range(size)]
        )

    def crossed(block):
        def pair(d):
            if d % SEAM == 0:
                return d, (d - 1) % size
            if d % SEAM == 1:
                return d, (d + 1) % size
            return d, (d + (-2 if d % 2 else 2)) % size

        return lax.ppermute(block, "dp", [pair(d) for d in range(size)])

    first = (lax.axis_index("dp") % SEAM < 2).astype(jnp.int32).reshape(1)

    def swap(block):
        return lax.ppermute(block, "dp", [(d, d ^ 1) for d in range(size)])

    def last(name, *operands):
        return call(
            last_kernel,
            name,
            (*tb, *operands),
            one,
            out_spec=HBM,
            scratch_shapes=[
                pltpu.VMEM((rows, width), F32),
                pltpu.SemaphoreType.DMA((pl.cdiv(width, COLUMNS),)),
            ],
        )

    def after(*values):
        return lax.optimization_barrier(values)

    near_txt = outward(text_embed)
    in_hbm = [
        pltpu.with_memory_space_constraint(raw, pltpu.HBM)
        for raw in (image_embed, text_embed)
    ]
    ihat, that, both, ihat_a, ihat_b, *rest = call(
        unit_kernel,
        "unit_rows",
        in_hbm,
        (one, one, shape(2 * rows), shape(rows - tail), shape(tail), *state, *state),
        scalars=0,
        spec=HBM,
        scratch_shapes=[
            pltpu.VMEM((2 * rows, width), F32),
            pltpu.SemaphoreType.DMA((2, PARTS)),
        ],
    )
    iinv, ihi, ilo, tinv, thi, tlo = rest
    img, txt = (ihi, ilo), (thi, tlo)
    near_img = outward(ihat)
    pair = swap(both)
    igrad, tgrad = call(own_kernel, "own_tiles", (*tb, *img, *txt), (one, one))

    that_late, igrad, tgrad = after(that, igrad, tgrad)
    far_txt = inward(that_late)
    near_txt, igrad = call(
        raw_kernel, "near_text", (*tb, *img, near_txt, igrad), (one, one)
    )
    near_txt, igrad, pair = after(near_txt, igrad, pair)
    send_a, send_b = call(
        choose_kernel,
        "choose_rows",
        (first, pair, ihat_a, ihat_b),
        (shape(rows - tail), shape(tail)),
        scalars=1,
    )
    far_img_a = crossed(send_a)
    far_img_b = crossed(send_b)
    cross_txt = swap(near_txt)
    igrad, tgrad = call(
        pair_kernel, "pair_tiles", (*tb, *img, *txt, pair, igrad, tgrad), (one, one)
    )
    igrad, inner_img = call(
        cross_kernel, "cross_text", (*tb, *img, cross_txt, igrad, ihat), (one, column)
    )

    near_img, igrad = after(near_img, igrad)
    cross_img = swap(near_img)
    tgrad = call(tile_kernel, "near_image", (*tb, *txt, near_img, tgrad), one)

    far_txt, igrad, tgrad = after(far_txt, igrad, tgrad)
    grad_image = last("last_text", *img, far_txt, igrad, ihat, inner_img, iinv)
    cross_img, grad_image = after(cross_img, grad_image)
    tgrad = call(tile_kernel, "cross_image", (*tb, *txt, cross_img, tgrad), one)
    tgrad, inner_txt = call(
        cross_kernel, "far_image", (*tb, *txt, far_img_a, tgrad, that), (one, column)
    )
    grad_text = last("last_image", *txt, far_img_b, tgrad, that, inner_txt, tinv)
    return grad_image, grad_text


def solution(mesh):
    return jax.shard_map(
        body,
        mesh=mesh,
        in_specs=(P("dp", None), P("dp", None), P(), P()),
        out_specs=(P("dp", None), P("dp", None)),
        check_vma=False,
    )
```

```python
import functools

import jax
import jax.numpy as jnp
from jax import lax
from jax.experimental import pallas as pl
from jax.experimental.pallas import tpu as pltpu
from jax.sharding import PartitionSpec as P

F32 = jnp.float32
BF16 = jnp.bfloat16
VMEM = pl.BlockSpec(memory_space=pltpu.VMEM)
SMEM = pl.BlockSpec(memory_space=pltpu.SMEM)
HBM = pl.BlockSpec(memory_space=pltpu.HBM)
PARTS = 4
COLUMNS = 256
SEAM = 128
HINTS = {"choose_rows": 1, "last_text": 1, "cross_image": 1, "far_image": 1}
NT = (((1,), (1,)), ((), ()))
NN = (((1,), (0,)), ((), ()))


def split(value):
    hi = value.astype(BF16)
    return hi, (value - hi.astype(F32)).astype(BF16)


def product(left, right, dims):
    mul = functools.partial(
        lax.dot_general, dimension_numbers=dims, preferred_element_type=F32
    )
    (lh, ll), (rh, rl) = left, right
    return mul(lh, rh) + (mul(lh, rl) + mul(ll, rh))


def unit(raw):
    inv = 1.0 / jnp.sqrt(jnp.sum(raw * raw, axis=1, keepdims=True) + 1e-06)
    return raw * inv, inv


def tile_grad(x, y, scale, bias, matching=False):
    logits = scale * product(x, y, NT) + bias
    if matching:
        diag = lax.broadcasted_iota(jnp.int32, logits.shape, 0) == (
            lax.broadcasted_iota(jnp.int32, logits.shape, 1)
        )
        sign = jnp.where(diag, -1.0, 1.0)
        coeff = sign * jax.nn.sigmoid(sign * logits)
    else:
        coeff = jax.nn.sigmoid(logits)
    return product(split(coeff), y, NN)


def unit_kernel(img_in, txt_in, ihat, that, both, ihat_a, ihat_b, *refs):
    (iinv, ihi, ilo, tinv, thi, tlo, raw, sems) = refs
    rows = ihat.shape[0]
    part = rows // PARTS
    copies = []
    for n, source in enumerate((img_in, txt_in)):
        for k in range(PARTS):
            copies.append(
                pltpu.make_async_copy(
                    source.at[pl.ds(k * part, part)],
                    raw.at[pl.ds(n * rows + k * part, part)],
                    sems.at[n, k],
                )
            )
    for copy in copies:
        copy.start()
    for n, (hat, inv, hi, lo) in enumerate(((ihat, iinv, ihi, ilo), (that, tinv, thi, tlo))):
        for copy in copies[n * PARTS : (n + 1) * PARTS]:
            copy.wait()
        hat[...], inv[...] = unit(raw[n * rows : (n + 1) * rows])
        both[n * rows : (n + 1) * rows] = hat[...]
        hi[...], lo[...] = split(hat[...])
        if n == 0:
            ihat_a[...] = hat[: ihat_a.shape[0]]
            ihat_b[...] = hat[ihat_a.shape[0] :]


def own_kernel(scale, bias, ihi, ilo, thi, tlo, igrad, tgrad):
    x, y = (ihi[...], ilo[...]), (thi[...], tlo[...])
    igrad[...] = tile_grad(x, y, scale[0], bias[0], True)
    tgrad[...] = tile_grad(y, x, scale[0], bias[0], True)


def tile_kernel(scale, bias, hi, lo, hat, grad, total):
    total[...] = grad[...] + tile_grad(
        (hi[...], lo[...]), split(hat[...]), scale[0], bias[0]
    )


def raw_kernel(scale, bias, hi, lo, raw, grad, hat, total):
    hat[...] = unit(raw[...])[0]
    tile_kernel(scale, bias, hi, lo, hat, grad, total)


def choose_kernel(first, both, own_a, own_b, out_a, out_b):
    cut = own_a.shape[0]

    @pl.when(first[0] != 0)
    def _():
        out_a[...] = both[:cut]
        out_b[...] = both[cut : cut + own_b.shape[0]]

    @pl.when(first[0] == 0)
    def _():
        out_a[...] = own_a[...]
        out_b[...] = own_b[...]


def pair_kernel(scale, bias, ihi, ilo, thi, tlo, both, igrad, tgrad, itotal, ttotal):
    rows = igrad.shape[0]
    tile_kernel(scale, bias, ihi, ilo, both.at[rows:], igrad, itotal)
    tile_kernel(scale, bias, thi, tlo, both.at[:rows], tgrad, ttotal)


def cross_kernel(scale, bias, hi, lo, hat, grad, own, total, inner):
    tile_kernel(scale, bias, hi, lo, hat, grad, total)
    inner[...] = jnp.sum(own[...] * total[...], axis=1, keepdims=True)


def stacked(hi, lo, y_hi, y_lo, scale, bias):
    rows = y_hi.shape[0]
    mul = functools.partial(lax.dot_general, preferred_element_type=F32)
    both = mul(hi, jnp.concatenate([y_hi, y_lo], axis=0), NT)
    dots = both[:, :rows] + (both[:, rows:] + mul(lo, y_hi, NT))
    coeff = jax.nn.sigmoid(scale * dots + bias)
    top, rest = split(coeff)
    left = jnp.concatenate([top, rest], axis=1)
    right = jnp.concatenate([y_hi, y_hi], axis=0)
    return dots, coeff, lambda here: (
        mul(left, right[:, here], NN) + mul(top, y_lo[:, here], NN)
    )


def last_kernel(scale, bias, hi, lo, hat, grad, own, inner, inv, out, part, sems):
    y = split(hat[...])
    if 2 * hat.shape[0] <= hi.shape[0]:
        dots, coeff, columns = stacked(hi[...], lo[...], *y, scale[0], bias[0])
    else:
        dots = product((hi[...], lo[...]), y, NT)
        coeff = jax.nn.sigmoid(scale[0] * dots + bias[0])
        halves = split(coeff)
        columns = lambda here: product(halves, [half[:, here] for half in y], NN)
    along = inner[...] + jnp.sum(coeff * dots, axis=1, keepdims=True)
    factor = scale[0] * inv[...]
    copies = []
    width = hat.shape[1]
    for at in range(0, width, COLUMNS):
        here = slice(at, min(at + COLUMNS, width))
        total = grad[:, here] + columns(here)
        part[:, here] = (total - own[:, here] * along) * factor
        wide = pl.ds(at, here.stop - at)
        copies.append(
            pltpu.make_async_copy(
                part.at[:, wide], out.at[:, wide], sems.at[at // COLUMNS]
            )
        )
        copies[-1].start()
    for copy in copies:
        copy.wait()


def call(kernel, name, operands, outs, scalars=2, spec=VMEM, out_spec=VMEM, **extra):
    return pl.pallas_call(
        kernel,
        name=name,
        out_shape=outs,
        in_specs=[SMEM] * scalars + [spec] * (len(operands) - scalars),
        out_specs=jax.tree.map(lambda _: out_spec, outs),
        compiler_params=pltpu.CompilerParams(vmem_limit_bytes=24 * 2**20),
        cost_estimate=pl.CostEstimate(
            flops=HINTS.get(name, 2 * 10**10), bytes_accessed=0, transcendentals=0
        ),
        **extra,
    )(*operands)


def body(image_embed, text_embed, logit_scale, logit_bias):
    rows, width = image_embed.shape
    size = lax.axis_size("dp")

    def shape(height, wide=width, kind=F32):
        return jax.ShapeDtypeStruct((height, wide), kind)

    one = shape(rows)
    tail = rows // 2
    column = shape(rows, 1)
    state = (column, shape(rows, kind=BF16), shape(rows, kind=BF16))
    tb = (logit_scale, logit_bias)

    def outward(block):
        return lax.ppermute(
            block, "dp", [(d, (d + (2 if d % 2 else -2)) % size) for d in range(size)]
        )

    def inward(block):
        return lax.ppermute(
            block, "dp", [(d, (d + (-2 if d % 2 else 2)) % size) for d in range(size)]
        )

    def crossed(block):
        def pair(d):
            if d % SEAM == 0:
                return d, (d - 1) % size
            if d % SEAM == 1:
                return d, (d + 1) % size
            return d, (d + (-2 if d % 2 else 2)) % size

        return lax.ppermute(block, "dp", [pair(d) for d in range(size)])

    first = (lax.axis_index("dp") % SEAM < 2).astype(jnp.int32).reshape(1)

    def swap(block):
        return lax.ppermute(block, "dp", [(d, d ^ 1) for d in range(size)])

    def last(name, *operands):
        return call(
            last_kernel,
            name,
            (*tb, *operands),
            one,
            out_spec=HBM,
            scratch_shapes=[
                pltpu.VMEM((rows, width), F32),
                pltpu.SemaphoreType.DMA((pl.cdiv(width, COLUMNS),)),
            ],
        )

    def after(*values):
        return lax.optimization_barrier(values)

    near_txt = outward(text_embed)
    in_hbm = [
        pltpu.with_memory_space_constraint(raw, pltpu.HBM)
        for raw in (image_embed, text_embed)
    ]
    ihat, that, both, ihat_a, ihat_b, *rest = call(
        unit_kernel,
        "unit_rows",
        in_hbm,
        (one, one, shape(2 * rows), shape(rows - tail), shape(tail), *state, *state),
        scalars=0,
        spec=HBM,
        scratch_shapes=[
            pltpu.VMEM((2 * rows, width), F32),
            pltpu.SemaphoreType.DMA((2, PARTS)),
        ],
    )
    iinv, ihi, ilo, tinv, thi, tlo = rest
    img, txt = (ihi, ilo), (thi, tlo)
    near_img = outward(ihat)
    pair = swap(both)
    igrad, tgrad = call(own_kernel, "own_tiles", (*tb, *img, *txt), (one, one))

    that_late, igrad, tgrad = after(that, igrad, tgrad)
    far_txt = inward(that_late)
    near_txt, igrad = call(
        raw_kernel, "near_text", (*tb, *img, near_txt, igrad), (one, one)
    )
    near_txt, igrad, pair = after(near_txt, igrad, pair)
    send_a, send_b = call(
        choose_kernel,
        "choose_rows",
        (first, pair, ihat_a, ihat_b),
        (shape(rows - tail), shape(tail)),
        scalars=1,
    )
    far_img_a = crossed(send_a)
    far_img_b = crossed(send_b)
    cross_txt = swap(near_txt)
    igrad, tgrad = call(
        pair_kernel, "pair_tiles", (*tb, *img, *txt, pair, igrad, tgrad), (one, one)
    )
    igrad, inner_img = call(
        cross_kernel, "cross_text", (*tb, *img, cross_txt, igrad, ihat), (one, column)
    )

    near_img, igrad = after(near_img, igrad)
    cross_img = swap(near_img)
    tgrad = call(tile_kernel, "near_image", (*tb, *txt, near_img, tgrad), one)

    far_txt, igrad, tgrad = after(far_txt, igrad, tgrad)
    grad_image = last("last_text", *img, far_txt, igrad, ihat, inner_img, iinv)
    cross_img, grad_image = after(cross_img, grad_image)
    tgrad = call(tile_kernel, "cross_image", (*tb, *txt, cross_img, tgrad), one)
    tgrad, inner_txt = call(
        cross_kernel, "far_image", (*tb, *txt, far_img_a, tgrad, that), (one, column)
    )
    grad_text = last("last_image", *txt, far_img_b, tgrad, that, inner_txt, tinv)
    return grad_image, grad_text


def solution(mesh):
    return jax.shard_map(
        body,
        mesh=mesh,
        in_specs=(P("dp", None), P("dp", None), P(), P()),
        out_specs=(P("dp", None), P("dp", None)),
        check_vma=False,
    )
```

```python
import functools

import jax
import jax.numpy as jnp
from jax import lax
from jax.experimental import pallas as pl
from jax.experimental.pallas import tpu as pltpu
from jax.sharding import PartitionSpec as P

F32 = jnp.float32
BF16 = jnp.bfloat16
VMEM = pl.BlockSpec(memory_space=pltpu.VMEM)
SMEM = pl.BlockSpec(memory_space=pltpu.SMEM)
HBM = pl.BlockSpec(memory_space=pltpu.HBM)
PARTS = 4
COLUMNS = 256
SEAM = 128
HINTS = {"last_text": 1, "cross_image": 1, "far_image": 1}
NT = (((1,), (1,)), ((), ()))
NN = (((1,), (0,)), ((), ()))


def split(value):
    hi = value.astype(BF16)
    return hi, (value - hi.astype(F32)).astype(BF16)


def product(left, right, dims):
    mul = functools.partial(
        lax.dot_general, dimension_numbers=dims, preferred_element_type=F32
    )
    (lh, ll), (rh, rl) = left, right
    return mul(lh, rh) + (mul(lh, rl) + mul(ll, rh))


def unit(raw):
    inv = 1.0 / jnp.sqrt(jnp.sum(raw * raw, axis=1, keepdims=True) + 1e-06)
    return raw * inv, inv


def tile_grad(x, y, scale, bias, matching=False):
    logits = scale * product(x, y, NT) + bias
    if matching:
        diag = lax.broadcasted_iota(jnp.int32, logits.shape, 0) == (
            lax.broadcasted_iota(jnp.int32, logits.shape, 1)
        )
        sign = jnp.where(diag, -1.0, 1.0)
        coeff = sign * jax.nn.sigmoid(sign * logits)
    else:
        coeff = jax.nn.sigmoid(logits)
    return product(split(coeff), y, NN)


def unit_kernel(img_in, txt_in, ihat, that, both, ihat_a, ihat_b, *refs):
    (iinv, ihi, ilo, tinv, thi, tlo, raw, sems) = refs
    rows = ihat.shape[0]
    part = rows // PARTS
    copies = []
    for n, source in enumerate((img_in, txt_in)):
        for k in range(PARTS):
            copies.append(
                pltpu.make_async_copy(
                    source.at[pl.ds(k * part, part)],
                    raw.at[pl.ds(n * rows + k * part, part)],
                    sems.at[n, k],
                )
            )
    for copy in copies:
        copy.start()
    for n, (hat, inv, hi, lo) in enumerate(((ihat, iinv, ihi, ilo), (that, tinv, thi, tlo))):
        for copy in copies[n * PARTS : (n + 1) * PARTS]:
            copy.wait()
        hat[...], inv[...] = unit(raw[n * rows : (n + 1) * rows])
        both[n * rows : (n + 1) * rows] = hat[...]
        hi[...], lo[...] = split(hat[...])
        if n == 0:
            ihat_a[...] = hat[: ihat_a.shape[0]]
            ihat_b[...] = hat[ihat_a.shape[0] :]


def own_kernel(scale, bias, ihi, ilo, thi, tlo, igrad, tgrad):
    x, y = (ihi[...], ilo[...]), (thi[...], tlo[...])
    igrad[...] = tile_grad(x, y, scale[0], bias[0], True)
    tgrad[...] = tile_grad(y, x, scale[0], bias[0], True)


def tile_kernel(scale, bias, hi, lo, hat, grad, total):
    total[...] = grad[...] + tile_grad(
        (hi[...], lo[...]), split(hat[...]), scale[0], bias[0]
    )


def raw_kernel(scale, bias, hi, lo, raw, grad, hat, total):
    hat[...] = unit(raw[...])[0]
    tile_kernel(scale, bias, hi, lo, hat, grad, total)


def pair_kernel(scale, bias, ihi, ilo, thi, tlo, both, igrad, tgrad, itotal, ttotal):
    rows = igrad.shape[0]
    tile_kernel(scale, bias, ihi, ilo, both.at[rows:], igrad, itotal)
    tile_kernel(scale, bias, thi, tlo, both.at[:rows], tgrad, ttotal)


def cross_kernel(scale, bias, hi, lo, hat, grad, own, total, inner):
    tile_kernel(scale, bias, hi, lo, hat, grad, total)
    inner[...] = jnp.sum(own[...] * total[...], axis=1, keepdims=True)


def stacked(hi, lo, y_hi, y_lo, scale, bias):
    rows = y_hi.shape[0]
    mul = functools.partial(lax.dot_general, preferred_element_type=F32)
    both = mul(hi, jnp.concatenate([y_hi, y_lo], axis=0), NT)
    dots = both[:, :rows] + (both[:, rows:] + mul(lo, y_hi, NT))
    coeff = jax.nn.sigmoid(scale * dots + bias)
    top, rest = split(coeff)
    left = jnp.concatenate([top, rest], axis=1)
    right = jnp.concatenate([y_hi, y_hi], axis=0)
    return dots, coeff, lambda here: (
        mul(left, right[:, here], NN) + mul(top, y_lo[:, here], NN)
    )


def last_kernel(scale, bias, hi, lo, hat, grad, own, inner, inv, out, part, sems):
    y = split(hat[...])
    if 2 * hat.shape[0] <= hi.shape[0]:
        dots, coeff, columns = stacked(hi[...], lo[...], *y, scale[0], bias[0])
    else:
        dots = product((hi[...], lo[...]), y, NT)
        coeff = jax.nn.sigmoid(scale[0] * dots + bias[0])
        halves = split(coeff)
        columns = lambda here: product(halves, [half[:, here] for half in y], NN)
    along = inner[...] + jnp.sum(coeff * dots, axis=1, keepdims=True)
    factor = scale[0] * inv[...]
    copies = []
    width = hat.shape[1]
    for at in range(0, width, COLUMNS):
        here = slice(at, min(at + COLUMNS, width))
        total = grad[:, here] + columns(here)
        part[:, here] = (total - own[:, here] * along) * factor
        wide = pl.ds(at, here.stop - at)
        copies.append(
            pltpu.make_async_copy(
                part.at[:, wide], out.at[:, wide], sems.at[at // COLUMNS]
            )
        )
        copies[-1].start()
    for copy in copies:
        copy.wait()


def call(kernel, name, operands, outs, scalars=2, spec=VMEM, out_spec=VMEM, **extra):
    return pl.pallas_call(
        kernel,
        name=name,
        out_shape=outs,
        in_specs=[SMEM] * scalars + [spec] * (len(operands) - scalars),
        out_specs=jax.tree.map(lambda _: out_spec, outs),
        compiler_params=pltpu.CompilerParams(vmem_limit_bytes=24 * 2**20),
        cost_estimate=pl.CostEstimate(
            flops=HINTS.get(name, 2 * 10**10), bytes_accessed=0, transcendentals=0
        ),
        **extra,
    )(*operands)


def body(image_embed, text_embed, logit_scale, logit_bias):
    rows, width = image_embed.shape
    size = lax.axis_size("dp")

    def shape(height, wide=width, kind=F32):
        return jax.ShapeDtypeStruct((height, wide), kind)

    one = shape(rows)
    tail = rows // 2
    column = shape(rows, 1)
    state = (column, shape(rows, kind=BF16), shape(rows, kind=BF16))
    tb = (logit_scale, logit_bias)

    def outward(block):
        return lax.ppermute(
            block, "dp", [(d, (d + (2 if d % 2 else -2)) % size) for d in range(size)]
        )

    def inward(block):
        return lax.ppermute(
            block, "dp", [(d, (d + (-2 if d % 2 else 2)) % size) for d in range(size)]
        )

    def crossed(block):
        def pair(d):
            if d % SEAM == 0:
                return d, (d - 1) % size
            if d % SEAM == 1:
                return d, (d + 1) % size
            return d, (d + (-2 if d % 2 else 2)) % size

        return lax.ppermute(block, "dp", [pair(d) for d in range(size)])

    first = lax.axis_index("dp") % SEAM < 2

    def swap(block):
        return lax.ppermute(block, "dp", [(d, d ^ 1) for d in range(size)])

    def last(name, *operands):
        return call(
            last_kernel,
            name,
            (*tb, *operands),
            one,
            out_spec=HBM,
            scratch_shapes=[
                pltpu.VMEM((rows, width), F32),
                pltpu.SemaphoreType.DMA((pl.cdiv(width, COLUMNS),)),
            ],
        )

    def after(*values):
        return lax.optimization_barrier(values)

    near_txt = outward(text_embed)
    in_hbm = [
        pltpu.with_memory_space_constraint(raw, pltpu.HBM)
        for raw in (image_embed, text_embed)
    ]
    ihat, that, both, ihat_a, ihat_b, *rest = call(
        unit_kernel,
        "unit_rows",
        in_hbm,
        (one, one, shape(2 * rows), shape(rows - tail), shape(tail), *state, *state),
        scalars=0,
        spec=HBM,
        scratch_shapes=[
            pltpu.VMEM((2 * rows, width), F32),
            pltpu.SemaphoreType.DMA((2, PARTS)),
        ],
    )
    iinv, ihi, ilo, tinv, thi, tlo = rest
    img, txt = (ihi, ilo), (thi, tlo)
    near_img = outward(ihat)
    pair = swap(both)
    igrad, tgrad = call(own_kernel, "own_tiles", (*tb, *img, *txt), (one, one))

    that_late, igrad, tgrad = after(that, igrad, tgrad)
    far_txt = inward(that_late)
    near_txt, igrad = call(
        raw_kernel, "near_text", (*tb, *img, near_txt, igrad), (one, one)
    )
    near_txt, igrad, pair = after(near_txt, igrad, pair)
    cut = rows - tail
    send_a = jnp.where(first, pair[:cut], ihat_a)
    send_b = jnp.where(first, pair[cut:rows], ihat_b)
    far_img_a = crossed(send_a)
    far_img_b = crossed(send_b)
    cross_txt = swap(near_txt)
    igrad, tgrad = call(
        pair_kernel, "pair_tiles", (*tb, *img, *txt, pair, igrad, tgrad), (one, one)
    )
    igrad, inner_img = call(
        cross_kernel, "cross_text", (*tb, *img, cross_txt, igrad, ihat), (one, column)
    )

    near_img, igrad = after(near_img, igrad)
    cross_img = swap(near_img)
    tgrad = call(tile_kernel, "near_image", (*tb, *txt, near_img, tgrad), one)

    far_txt, igrad, tgrad = after(far_txt, igrad, tgrad)
    grad_image = last("last_text", *img, far_txt, igrad, ihat, inner_img, iinv)
    cross_img, grad_image = after(cross_img, grad_image)
    tgrad = call(tile_kernel, "cross_image", (*tb, *txt, cross_img, tgrad), one)
    tgrad, inner_txt = call(
        cross_kernel, "far_image", (*tb, *txt, far_img_a, tgrad, that), (one, column)
    )
    grad_text = last("last_image", *txt, far_img_b, tgrad, that, inner_txt, tinv)
    return grad_image, grad_text


def solution(mesh):
    return jax.shard_map(
        body,
        mesh=mesh,
        in_specs=(P("dp", None), P("dp", None), P(), P()),
        out_specs=(P("dp", None), P("dp", None)),
        check_vma=False,
    )
```

```python
import functools

import jax
import jax.numpy as jnp
from jax import lax
from jax.experimental import pallas as pl
from jax.experimental.pallas import tpu as pltpu
from jax.sharding import PartitionSpec as P

F32 = jnp.float32
BF16 = jnp.bfloat16
VMEM = pl.BlockSpec(memory_space=pltpu.VMEM)
SMEM = pl.BlockSpec(memory_space=pltpu.SMEM)
HBM = pl.BlockSpec(memory_space=pltpu.HBM)
PARTS = 4
COLUMNS = 384
HINTS = {"last_text": 1, "cross_image": 1, "far_image": 1}
NT = (((1,), (1,)), ((), ()))
NN = (((1,), (0,)), ((), ()))


def split(value):
    hi = value.astype(BF16)
    return hi, (value - hi.astype(F32)).astype(BF16)


def product(left, right, dims):
    mul = functools.partial(
        lax.dot_general, dimension_numbers=dims, preferred_element_type=F32
    )
    (lh, ll), (rh, rl) = left, right
    return mul(lh, rh) + (mul(lh, rl) + mul(ll, rh))


def unit(raw):
    inv = 1.0 / jnp.sqrt(jnp.sum(raw * raw, axis=1, keepdims=True) + 1e-06)
    return raw * inv, inv


def tile_grad(x, y, scale, bias, matching=False):
    logits = scale * product(x, y, NT) + bias
    if matching:
        diag = lax.broadcasted_iota(jnp.int32, logits.shape, 0) == (
            lax.broadcasted_iota(jnp.int32, logits.shape, 1)
        )
        sign = jnp.where(diag, -1.0, 1.0)
        coeff = sign * jax.nn.sigmoid(sign * logits)
    else:
        coeff = jax.nn.sigmoid(logits)
    return product(split(coeff), y, NN)


def unit_kernel(img_in, txt_in, ihat, that, both, ihat_a, ihat_b, *refs):
    (iinv, ihi, ilo, tinv, thi, tlo, raw, sems) = refs
    rows = ihat.shape[0]
    part = rows // PARTS
    copies = []
    for n, source in enumerate((img_in, txt_in)):
        for k in range(PARTS):
            copies.append(
                pltpu.make_async_copy(
                    source.at[pl.ds(k * part, part)],
                    raw.at[pl.ds(n * rows + k * part, part)],
                    sems.at[n, k],
                )
            )
    for copy in copies:
        copy.start()
    for n, (hat, inv, hi, lo) in enumerate(((ihat, iinv, ihi, ilo), (that, tinv, thi, tlo))):
        for copy in copies[n * PARTS : (n + 1) * PARTS]:
            copy.wait()
        hat[...], inv[...] = unit(raw[n * rows : (n + 1) * rows])
        both[n * rows : (n + 1) * rows] = hat[...]
        hi[...], lo[...] = split(hat[...])
        if n == 0:
            ihat_a[...] = hat[: ihat_a.shape[0]]
            ihat_b[...] = hat[ihat_a.shape[0] :]


def own_kernel(scale, bias, ihi, ilo, thi, tlo, igrad, tgrad):
    x, y = (ihi[...], ilo[...]), (thi[...], tlo[...])
    igrad[...] = tile_grad(x, y, scale[0], bias[0], True)
    tgrad[...] = tile_grad(y, x, scale[0], bias[0], True)


def tile_kernel(scale, bias, hi, lo, hat, grad, total):
    total[...] = grad[...] + tile_grad(
        (hi[...], lo[...]), split(hat[...]), scale[0], bias[0]
    )


def raw_kernel(scale, bias, hi, lo, raw, grad, hat, total):
    hat[...] = unit(raw[...])[0]
    tile_kernel(scale, bias, hi, lo, hat, grad, total)


def pair_kernel(scale, bias, ihi, ilo, thi, tlo, both, igrad, tgrad, *outs):
    itotal, ttotal, passed = outs
    rows = igrad.shape[0]
    passed[...] = both[rows - passed.shape[0] : rows]
    tile_kernel(scale, bias, ihi, ilo, both.at[rows:], igrad, itotal)
    tile_kernel(scale, bias, thi, tlo, both.at[:rows], tgrad, ttotal)


def cross_kernel(scale, bias, hi, lo, hat, grad, own, total, inner):
    tile_kernel(scale, bias, hi, lo, hat, grad, total)
    inner[...] = jnp.sum(own[...] * total[...], axis=1, keepdims=True)


def stacked(hi, lo, y_hi, y_lo, scale, bias):
    rows = y_hi.shape[0]
    mul = functools.partial(lax.dot_general, preferred_element_type=F32)
    both = mul(hi, jnp.concatenate([y_hi, y_lo], axis=0), NT)
    dots = both[:, :rows] + (both[:, rows:] + mul(lo, y_hi, NT))
    coeff = jax.nn.sigmoid(scale * dots + bias)
    top, rest = split(coeff)
    left = jnp.concatenate([top, rest], axis=1)
    right = jnp.concatenate([y_hi, y_hi], axis=0)
    return dots, coeff, lambda here: (
        mul(left, right[:, here], NN) + mul(top, y_lo[:, here], NN)
    )


def last_kernel(hats, scale, bias, hi, lo, *refs):
    grad, own, inner, inv, out, part, sems = refs[hats:]
    hat = refs[0][...]
    for more in refs[1:hats]:
        hat += more[...]
    y = split(hat)
    if 2 * hat.shape[0] <= hi.shape[0]:
        dots, coeff, columns = stacked(hi[...], lo[...], *y, scale[0], bias[0])
    else:
        dots = product((hi[...], lo[...]), y, NT)
        coeff = jax.nn.sigmoid(scale[0] * dots + bias[0])
        halves = split(coeff)
        columns = lambda here: product(halves, [half[:, here] for half in y], NN)
    along = inner[...] + jnp.sum(coeff * dots, axis=1, keepdims=True)
    factor = scale[0] * inv[...]
    copies = []
    width = hat.shape[1]
    for at in range(0, width, COLUMNS):
        here = slice(at, min(at + COLUMNS, width))
        total = grad[:, here] + columns(here)
        part[:, here] = (total - own[:, here] * along) * factor
        wide = pl.ds(at, here.stop - at)
        copies.append(
            pltpu.make_async_copy(
                part.at[:, wide], out.at[:, wide], sems.at[at // COLUMNS]
            )
        )
        copies[-1].start()
    for copy in copies:
        copy.wait()


def call(kernel, name, operands, outs, scalars=2, spec=VMEM, out_spec=VMEM, **extra):
    return pl.pallas_call(
        kernel,
        name=name,
        out_shape=outs,
        in_specs=[SMEM] * scalars + [spec] * (len(operands) - scalars),
        out_specs=jax.tree.map(lambda _: out_spec, outs),
        compiler_params=pltpu.CompilerParams(vmem_limit_bytes=24 * 2**20),
        cost_estimate=pl.CostEstimate(
            flops=HINTS.get(name, 2 * 10**10), bytes_accessed=0, transcendentals=0
        ),
        **extra,
    )(*operands)


def body(image_embed, text_embed, logit_scale, logit_bias):
    rows, width = image_embed.shape
    size = lax.axis_size("dp")

    def shape(height, wide=width, kind=F32):
        return jax.ShapeDtypeStruct((height, wide), kind)

    one = shape(rows)
    tail = rows // 2
    column = shape(rows, 1)
    state = (column, shape(rows, kind=BF16), shape(rows, kind=BF16))
    tb = (logit_scale, logit_bias)

    def outward(block):
        return lax.ppermute(
            block, "dp", [(d, (d + (2 if d % 2 else -2)) % size) for d in range(size)]
        )

    def inward(block, skip=()):
        pairs = [(d, (d + (-2 if d % 2 else 2)) % size) for d in range(size)]
        return lax.ppermute(block, "dp", [pair for pair in pairs if pair not in skip])

    def swap(block):
        return lax.ppermute(block, "dp", [(d, d ^ 1) for d in range(size)])

    def last(name, hats, *operands):
        return call(
            functools.partial(last_kernel, hats),
            name,
            (*tb, *operands),
            one,
            out_spec=HBM,
            scratch_shapes=[
                pltpu.VMEM((rows, width), F32),
                pltpu.SemaphoreType.DMA((pl.cdiv(width, COLUMNS),)),
            ],
        )

    def after(*values):
        return lax.optimization_barrier(values)

    near_txt = outward(text_embed)
    in_hbm = [
        pltpu.with_memory_space_constraint(raw, pltpu.HBM)
        for raw in (image_embed, text_embed)
    ]
    ihat, that, both, ihat_a, ihat_b, *rest = call(
        unit_kernel,
        "unit_rows",
        in_hbm,
        (one, one, shape(2 * rows), shape(rows - tail), shape(tail), *state, *state),
        scalars=0,
        spec=HBM,
        scratch_shapes=[
            pltpu.VMEM((2 * rows, width), F32),
            pltpu.SemaphoreType.DMA((2, PARTS)),
        ],
    )
    iinv, ihi, ilo, tinv, thi, tlo = rest
    img, txt = (ihi, ilo), (thi, tlo)
    near_img = outward(ihat)
    pair = swap(both)
    igrad, tgrad = call(own_kernel, "own_tiles", (*tb, *img, *txt), (one, one))

    that_late, igrad, tgrad = after(that, igrad, tgrad)
    far_txt = inward(that_late)
    near_txt, igrad = call(
        raw_kernel, "near_text", (*tb, *img, near_txt, igrad), (one, one)
    )
    ihat_a, ihat_b, near_txt, igrad = after(ihat_a, ihat_b, near_txt, igrad)
    far_img_a = inward(ihat_a)
    far_img_b = inward(ihat_b, [(1, size - 1)])
    cross_txt = swap(near_txt)
    igrad, tgrad, passed = call(
        pair_kernel,
        "pair_tiles",
        (*tb, *img, *txt, pair, igrad, tgrad),
        (one, one, shape(tail)),
    )
    far_img_c = lax.ppermute(passed, "dp", [(0, size - 1)])
    igrad, inner_img = call(
        cross_kernel, "cross_text", (*tb, *img, cross_txt, igrad, ihat), (one, column)
    )

    near_img, igrad = after(near_img, igrad)
    cross_img = swap(near_img)
    tgrad = call(tile_kernel, "near_image", (*tb, *txt, near_img, tgrad), one)

    far_txt, igrad, tgrad = after(far_txt, igrad, tgrad)
    grad_image = last("last_text", 1, *img, far_txt, igrad, ihat, inner_img, iinv)
    cross_img, grad_image = after(cross_img, grad_image)
    tgrad = call(tile_kernel, "cross_image", (*tb, *txt, cross_img, tgrad), one)
    tgrad, inner_txt = call(
        cross_kernel, "far_image", (*tb, *txt, far_img_a, tgrad, that), (one, column)
    )
    grad_text = last(
        "last_image", 2, *txt, far_img_b, far_img_c, tgrad, that, inner_txt, tinv
    )
    return grad_image, grad_text


def solution(mesh):
    return jax.shard_map(
        body,
        mesh=mesh,
        in_specs=(P("dp", None), P("dp", None), P(), P()),
        out_specs=(P("dp", None), P("dp", None)),
        check_vma=False,
    )
```
